128 devices in a mesh: tile: 32 (over y, z, core), cam: 4 (over x).
Axes of the slice: x: 4, y: 4, z: 4, core: 2. Of those that a mesh axis runs over, the one named last changes fastest.
Arguments:
- pixels: bfloat16 [256, 4096, 128], P('cam', 'tile'), may hold values from -6 to 6
- pixel_hidden: bfloat16 [256, 4096, 128], P('cam', 'tile'), may hold values from -6 to 6
- pixel_upstream: bfloat16 [256, 4096, 128], P('cam', 'tile'), may hold values from -1.5 to 1.5
- points: bfloat16 [262144, 128], P(('tile', 'cam')), may hold values from -6 to 6
- point_hidden: bfloat16 [262144, 128], P(('tile', 'cam')), may hold values from -6 to 6
- point_upstream: bfloat16 [262144, 128], P(('tile', 'cam')), may hold values from -1.5 to 1.5
- mixing: bfloat16 [4096, 256, 384], P(('tile', 'cam')), may hold values from -0.3125 to 0.3125
- neighbors: int32 [4096, 6], P(('tile', 'cam')), may hold values from 0 to 255
- send_list: int32 [128, 128, 2], P(('tile', 'cam')), may hold values from 0 to 31
- pixel_weight: bfloat16 [128, 128], replicated, may hold values from -0.5 to 0.5
- point_weight: bfloat16 [128, 128], replicated, may hold values from -0.5 to 0.5
- kernel: float32 [3, 3, 128], replicated, may hold values from -2 to 2
Outputs:
- pixel_gradient: bfloat16 [256, 4096, 128], P('cam', 'tile')
- point_gradient: bfloat16 [262144, 128], P(('tile', 'cam'))
- mixing_gradient: bfloat16 [4096, 256, 384], P(('tile', 'cam'))
The draws below stay inside these ranges and needn't reach their ends.
Inputs may be any that keep to these rules, and one draw needn't show every extreme that they name: `neighbors`: entry s names slot s % 2 of the slots filled by device s // 2. `send_list`: entry [o, d, s] is the block of device o, counted within that device, that fills slot s from device o at device d.
All inputs are finite; a program needn't handle non-finite values.
Results may differ from the reference program's by a relative error of at most 0.0054.
Values may be sent and summed in bfloat16 or wider, within the bound.
No kernel may reach another device: no remote copies, remote signals or barrier semaphores. Data moves between devices by JAX's collectives and lax.ppermute only.
A program may use at most 192 MiB of HBM per device.

```python
import jax
import jax.numpy as jnp
from jax import lax

C = 128
ROWS_DEV = 64
COLS_DEV = 128
WIDTH = 512
K = 6
BS = 64
CAP = 2
BLK_DEV = 32
PB = 32
PIXB = 256
H = 256
CAMS = 8
SLOTS = 256
BLOCKS = 4096
POINTS = 262144
N_TILE = 32
N_CAM = 4
DEVICES = 128


def with_ends(result, stream_key, low, top_value):
    extent = result.shape
    index_at = [jax.random.randint(jax.random.fold_in(stream_key, axis), (), 0, extent[axis]) for axis in range(len(extent))]
    result = result.at[tuple(index_at)].set(low)
    longest = extent.index(max(extent))
    index_at[longest] = (index_at[longest] + 1) % extent[longest]
    return result.at[tuple(index_at)].set(top_value)


def levels(stream_key, extent, shards, least, high):
    gain = 1.0
    for dim, parts in shards:
        draws = jax.random.uniform(jax.random.fold_in(jax.random.fold_in(stream_key, 6), dim), (parts,), jnp.float32, least / len(shards), high / len(shards))
        gain = gain * jnp.repeat(jnp.exp(draws), extent[dim] // parts).reshape((-1,) + (1,) * (len(extent) - 1 - dim))
    return gain


def normal_values(key, shape, scale, reach, shards=(), held_as=jnp.bfloat16):
    gain = levels(key, shape, shards, -0.22, 0.18) if shards else 1.0
    array = jax.random.normal(key, shape, jnp.float32) * scale * gain
    return jnp.minimum(jnp.maximum(array, -reach), reach).astype(held_as)


def setup_inputs(seed: int = 0) -> dict:
    splits = jax.random.split(jax.random.key(seed), 13)
    return {
        "pixels": normal_values(splits[0], (H, CAMS * WIDTH, C), 1.0, 6.0, ((0, 4), (1, 32))),
        "pixel_hidden": normal_values(splits[1], (H, CAMS * WIDTH, C), 1.5, 6.0, ((0, 4), (1, 32))),
        "pixel_upstream": normal_values(splits[2], (H, CAMS * WIDTH, C), 0.25, 1.5, ((0, 4), (1, 32))),
        "points": normal_values(splits[3], (POINTS, C), 1.0, 6.0, ((0, 128),)),
        "point_hidden": normal_values(splits[4], (POINTS, C), 1.5, 6.0, ((0, 128),)),
        "point_upstream": normal_values(splits[5], (POINTS, C), 0.25, 1.5, ((0, 128),)),
        "mixing": normal_values(splits[6], (DEVICES * PB, PIXB, K * BS), (K * BS) ** -0.5, 0.3125, ((0, 128),)),
        "neighbors": with_ends(jax.random.randint(splits[7], (DEVICES * PB, K), 0, SLOTS), jax.random.fold_in(splits[7], 1), 0, SLOTS - 1).astype(jnp.int32),
        "send_list": with_ends(jax.random.randint(splits[8], (DEVICES, DEVICES, CAP), 0, BLK_DEV), jax.random.fold_in(splits[8], 1), 0, BLK_DEV - 1).astype(jnp.int32),
        "pixel_weight": normal_values(splits[9], (C, C), C ** -0.5, 0.5),
        "point_weight": normal_values(splits[10], (C, C), C ** -0.5, 0.5),
        "kernel": normal_values(splits[11], (3, 3, C), 0.5, 2.0, (), jnp.float32),
    }


def silu_slope(hidden):
    argument = hidden.astype(jnp.float32)
    logistic = jax.nn.sigmoid(argument)
    return logistic * (1.0 + argument * (1.0 - logistic))


def tile_blocks(field_map):
    shaped = field_map.reshape(N_CAM, ROWS_DEV, N_TILE, COLS_DEV, C)
    shaped = jnp.transpose(shaped, (2, 0, 1, 3, 4))
    return shaped.reshape(N_TILE * N_CAM, PB, PIXB, C)


def untile_blocks(blocks):
    shaped = blocks.reshape(N_TILE, N_CAM, ROWS_DEV, COLS_DEV, C)
    shaped = jnp.transpose(shaped, (1, 2, 0, 3, 4))
    return shaped.reshape(H, CAMS * WIDTH, C)


def conv_back(slope_map, kernel):
    rolled = jnp.roll(slope_map.astype(jnp.float32), COLS_DEV, axis=1)
    shaped = rolled.reshape(H, CAMS, WIDTH, C)
    padded = jnp.pad(shaped, ((1, 1), (0, 0), (1, 1), (0, 0)))
    running = jnp.zeros((H, CAMS, WIDTH, C), jnp.float32)
    for row_shift in range(3):
        for col_shift in range(3):
            window = padded[2 - row_shift:2 - row_shift + H, :, 2 - col_shift:2 - col_shift + WIDTH, :]
            running = running + kernel[row_shift, col_shift] * window
    return jnp.roll(running.reshape(H, CAMS * WIDTH, C), -COLS_DEV, axis=1)


def reference(pixels, pixel_hidden, pixel_upstream, points, point_hidden, point_upstream, mixing, neighbors, send_list, pixel_weight, point_weight, kernel):
    devices = N_TILE * N_CAM
    pixel_slope = (pixel_upstream.astype(jnp.float32) * silu_slope(pixel_hidden)).astype(jnp.bfloat16)
    point_slope = (point_upstream.astype(jnp.float32) * silu_slope(point_hidden)).astype(jnp.bfloat16)
    mixed_slope = jnp.dot(pixel_slope.reshape(H * CAMS * WIDTH, C), pixel_weight.T, preferred_element_type=jnp.float32)
    mixed_slope = mixed_slope.astype(jnp.bfloat16).reshape(H, CAMS * WIDTH, C)
    owners = (neighbors // CAP).astype(jnp.int32)
    slot_index = (neighbors % CAP).astype(jnp.int32)
    target = (jnp.arange(devices * PB, dtype=jnp.int32) // PB)[:, None]
    chosen = (owners * BLK_DEV + send_list[owners, target, slot_index]).astype(jnp.int32).reshape(devices, PB, K)
    point_blocks = points.reshape(BLOCKS, BS, C)
    slope_blocks = point_slope.reshape(BLOCKS, BS, C)
    mixing_tiles = mixing.reshape(devices, PB, PIXB, K * BS)
    inputs = (chosen, mixing_tiles, tile_blocks(pixels), tile_blocks(mixed_slope))

    def visit_device(returned, parcel):
        block_index, weights, pixel_tile, mixed_tile = parcel
        gathered = point_blocks[block_index.reshape(-1)].reshape(PB, K * BS, C).astype(jnp.float32)
        gathered_slope = slope_blocks[block_index.reshape(-1)].reshape(PB, K * BS, C).astype(jnp.float32)
        mixing_wide = weights.astype(jnp.float32)
        mixed_wide = mixed_tile.astype(jnp.float32)
        mixing_grad = jnp.einsum("qpc,qjc->qpj", mixed_wide, gathered) + jnp.einsum("qpc,qjc->qpj", pixel_tile.astype(jnp.float32), gathered_slope)
        pixel_term = jnp.einsum("qpj,qjc->qpc", mixing_wide, gathered_slope)
        point_term = jnp.einsum("qpj,qpc->qjc", mixing_wide, mixed_wide).reshape(PB * K, BS, C)
        returned = returned.at[block_index.reshape(-1)].add(point_term)
        return returned, (mixing_grad.astype(jnp.bfloat16), pixel_term)

    returned, outputs = lax.scan(visit_device, jnp.zeros((BLOCKS, BS, C), jnp.float32), inputs)
    mixing_grads, pixel_terms = outputs
    pixel_gradient = (pixel_upstream.astype(jnp.float32) + conv_back(pixel_slope, kernel) + untile_blocks(pixel_terms)).astype(jnp.bfloat16)
    point_gradient = (point_upstream.astype(jnp.float32) + jnp.dot(point_slope, point_weight.T, preferred_element_type=jnp.float32) + returned.reshape(POINTS, C)).astype(jnp.bfloat16)
    mixing_gradient = mixing_grads.reshape(devices * PB, PIXB, K * BS)
    return (pixel_gradient, point_gradient, mixing_gradient)
```

```python
import functools

import jax
import jax.numpy as jnp
from jax import lax
from jax.experimental import pallas as pl
from jax.experimental.pallas import tpu as pltpu
from jax.sharding import PartitionSpec as P

C = 128
ROWS_DEV = 64
COLS_DEV = 128
K = 6
BS = 64
CAP = 2
BLK_DEV = 32
PB = 32
PIXB = 256
STRIPS = 4
MIB = 1024 * 1024
VMEM = 60 * MIB
DESTS = 8
OWNERS = 8


def slope_of(upstream, hidden):
    argument = hidden.astype(jnp.float32)
    logistic = jax.nn.sigmoid(argument)
    slope = logistic * (1.0 + argument * (1.0 - logistic))
    return (upstream.astype(jnp.float32) * slope).astype(jnp.bfloat16)


def pack_kernel(targets, points, hidden, upstream, out, slope):
    step = pl.program_id(0)

    @pl.when(step == 0)
    def _():
        def body(b, carry):
            slope[b] = slope_of(upstream[b], hidden[b])
            return carry

        lax.fori_loop(0, BLK_DEV, body, 0)

    for d in range(DESTS):
        for s in range(CAP):
            block = targets[(step * DESTS + d) * CAP + s]
            out[d, s] = points[block]
            out[d, CAP + s] = slope[block]


def pack(targets, points, hidden, upstream, devices):
    whole = pl.BlockSpec((BLK_DEV, BS, C), lambda i, t: (0, 0, 0))
    return pl.pallas_call(
        pack_kernel,
        grid_spec=pltpu.PrefetchScalarGridSpec(
            num_scalar_prefetch=1,
            grid=(devices // DESTS,),
            in_specs=[whole, whole, whole],
            out_specs=[
                pl.BlockSpec((DESTS, 2 * CAP, BS, C), lambda i, t: (i, 0, 0, 0)),
                whole,
            ],
        ),
        out_shape=[
            jax.ShapeDtypeStruct((devices, 2 * CAP, BS, C), jnp.bfloat16),
            jax.ShapeDtypeStruct((BLK_DEV, BS, C), jnp.bfloat16),
        ],
        compiler_params=pltpu.CompilerParams(vmem_limit_bytes=VMEM),
        cost_estimate=pl.CostEstimate(flops=10 * MIB, bytes_accessed=12 * MIB, transcendentals=0),
        name="pack",
    )(targets, points, hidden, upstream)


def pixel_kernel(
    neighbors, hidden, upstream, mixing, weight, slope, mixed, sums, first, last, total
):
    q = pl.program_id(0)

    @pl.when(q == 0)
    def _():
        total[...] = jnp.zeros_like(total)

    values = slope_of(upstream[...], hidden[...])
    slope[...] = values
    wide = values.astype(jnp.float32)
    for r in range(2):
        first[pl.ds(2 * q + r, 1), :] = wide[r, 0:1, :]
        last[pl.ds(2 * q + r, 1), :] = wide[r, COLS_DEV - 1 : COLS_DEV, :]
    projected = lax.dot_general(
        values.reshape(PIXB, C),
        weight[...],
        (((1,), (1,)), ((), ())),
        preferred_element_type=jnp.float32,
    ).astype(jnp.bfloat16)
    mixed[0] = projected
    term = lax.dot_general(
        mixing[0], projected, (((0,), (0,)), ((), ())), preferred_element_type=jnp.float32
    )
    for k in range(K):
        slot = neighbors[q * K + k]
        total[slot] += term[k * BS : (k + 1) * BS]

    @pl.when(q == PB - 1)
    def _():
        def body(i, carry):
            sums[i] = total[i].astype(jnp.bfloat16)
            return carry

        lax.fori_loop(0, total.shape[0], body, 0)


def pixel_part(neighbors, hidden, upstream, mixing, weight, slots):
    rows = pl.BlockSpec((2, COLS_DEV, C), lambda q, n: (q, 0, 0))
    return pl.pallas_call(
        pixel_kernel,
        grid_spec=pltpu.PrefetchScalarGridSpec(
            num_scalar_prefetch=1,
            grid=(PB,),
            in_specs=[
                rows,
                rows,
                pl.BlockSpec((1, PIXB, K * BS), lambda q, n: (q, 0, 0)),
                pl.BlockSpec((C, C), lambda q, n: (0, 0)),
            ],
            out_specs=[
                rows,
                pl.BlockSpec((1, PIXB, C), lambda q, n: (q, 0, 0)),
                pl.BlockSpec((slots, BS, C), lambda q, n: (0, 0, 0)),
                pl.BlockSpec((ROWS_DEV, C), lambda q, n: (0, 0)),
                pl.BlockSpec((ROWS_DEV, C), lambda q, n: (0, 0)),
            ],
            scratch_shapes=[pltpu.VMEM((slots, BS, C), jnp.float32)],
        ),
        out_shape=[
            jax.ShapeDtypeStruct((ROWS_DEV, COLS_DEV, C), jnp.bfloat16),
            jax.ShapeDtypeStruct((PB, PIXB, C), jnp.bfloat16),
            jax.ShapeDtypeStruct((slots, BS, C), jnp.bfloat16),
            jax.ShapeDtypeStruct((ROWS_DEV, C), jnp.float32),
            jax.ShapeDtypeStruct((ROWS_DEV, C), jnp.float32),
        ],
        compiler_params=pltpu.CompilerParams(vmem_limit_bytes=VMEM),
        cost_estimate=pl.CostEstimate(
            flops=1200 * MIB, bytes_accessed=18 * MIB, transcendentals=MIB
        ),
        name="pixel_part",
    )(neighbors, hidden, upstream, mixing, weight)


def main_kernel(
    neighbors, incoming, mixed, pixels, mixing, upstream, padded, left, right, kernel,
    mixing_gradient, pixel_gradient, left_side, right_side,
):
    q = pl.program_id(0)
    for k in range(K):
        slot = neighbors[q * K + k]
        owner = lax.div(slot, CAP)
        place = lax.rem(slot, CAP)
        right_side[k * BS : (k + 1) * BS, 0:C] = incoming[owner, place]
        right_side[k * BS : (k + 1) * BS, C : 2 * C] = incoming[owner, CAP + place]
    left_side[:, 0:C] = mixed[0]
    left_side[:, C : 2 * C] = pixels[...].reshape(PIXB, C)
    mixing_gradient[0] = lax.dot_general(
        left_side[...],
        right_side[...],
        (((1,), (1,)), ((), ())),
        preferred_element_type=jnp.float32,
    ).astype(jnp.bfloat16)
    term = jnp.dot(mixing[0], right_side[:, C : 2 * C], preferred_element_type=jnp.float32)
    column = lax.broadcasted_iota(jnp.int32, (COLS_DEV, C), 0)
    for r in range(2):
        row = 2 * q + r
        total = upstream[r].astype(jnp.float32) + term[r * COLS_DEV : (r + 1) * COLS_DEV]
        sides = []
        for e in range(3):
            part = None
            edge = None
            for a in range(3):
                gain = kernel[a, e : e + 1, :]
                piece = padded[row + 2 - a].astype(jnp.float32) * gain
                part = piece if part is None else part + piece
                if e != 1:
                    rim = right if e == 0 else left
                    corner = rim[pl.ds(row + 2 - a, 1), :] * gain
                    edge = corner if edge is None else edge + corner
            sides.append((part, edge))
        total = total + sides[1][0]
        ahead = pltpu.roll(sides[0][0], COLS_DEV - 1, 0)
        total = total + jnp.where(column == COLS_DEV - 1, sides[0][1], ahead)
        behind = pltpu.roll(sides[2][0], 1, 0)
        total = total + jnp.where(column == 0, sides[2][1], behind)
        pixel_gradient[r] = total.astype(jnp.bfloat16)


def main_part(neighbors, incoming, mixed, pixels, mixing, upstream, padded, left, right, kernel):
    rows = pl.BlockSpec((2, COLS_DEV, C), lambda q, n: (q, 0, 0))
    once = pl.Buffered(1)
    return pl.pallas_call(
        main_kernel,
        grid_spec=pltpu.PrefetchScalarGridSpec(
            num_scalar_prefetch=1,
            grid=(PB,),
            in_specs=[
                pl.BlockSpec(incoming.shape, lambda q, n: (0, 0, 0, 0), pipeline_mode=once),
                pl.BlockSpec((1, PIXB, C), lambda q, n: (q, 0, 0)),
                rows,
                pl.BlockSpec((1, PIXB, K * BS), lambda q, n: (q, 0, 0)),
                rows,
                pl.BlockSpec(padded.shape, lambda q, n: (0, 0, 0), pipeline_mode=once),
                pl.BlockSpec(left.shape, lambda q, n: (0, 0)),
                pl.BlockSpec(right.shape, lambda q, n: (0, 0)),
                pl.BlockSpec((3, 3, C), lambda q, n: (0, 0, 0)),
            ],
            out_specs=[
                pl.BlockSpec((1, PIXB, K * BS), lambda q, n: (q, 0, 0)),
                rows,
            ],
            scratch_shapes=[
                pltpu.VMEM((PIXB, 2 * C), jnp.bfloat16),
                pltpu.VMEM((K * BS, 2 * C), jnp.bfloat16),
            ],
        ),
        out_shape=[
            jax.ShapeDtypeStruct((PB, PIXB, K * BS), jnp.bfloat16),
            jax.ShapeDtypeStruct((ROWS_DEV, COLS_DEV, C), jnp.bfloat16),
        ],
        compiler_params=pltpu.CompilerParams(vmem_limit_bytes=VMEM),
        cost_estimate=pl.CostEstimate(
            flops=2600 * MIB, bytes_accessed=30 * MIB, transcendentals=0
        ),
        name="main_part",
    )(neighbors, incoming, mixed, pixels, mixing, upstream, padded, left, right, kernel)


def return_kernel(targets, received, base, out, total):
    step = pl.program_id(0)

    @pl.when(step == 0)
    def _():
        total[...] = base[...]

    for o in range(OWNERS):
        for s in range(CAP):
            block = targets[(step * OWNERS + o) * CAP + s]
            total[block] += received[o, s].astype(jnp.float32)

    @pl.when(step == pl.num_programs(0) - 1)
    def _():
        out[...] = total[...].astype(jnp.bfloat16)


def return_part(targets, received, base):
    devices = received.shape[0]
    whole = pl.BlockSpec((BLK_DEV, BS, C), lambda i, t: (0, 0, 0))
    return pl.pallas_call(
        return_kernel,
        grid_spec=pltpu.PrefetchScalarGridSpec(
            num_scalar_prefetch=1,
            grid=(devices // OWNERS,),
            in_specs=[
                pl.BlockSpec((OWNERS, CAP, BS, C), lambda i, t: (i, 0, 0, 0)),
                whole,
            ],
            out_specs=whole,
            scratch_shapes=[pltpu.VMEM((BLK_DEV, BS, C), jnp.float32)],
        ),
        out_shape=jax.ShapeDtypeStruct((BLK_DEV, BS, C), jnp.bfloat16),
        compiler_params=pltpu.CompilerParams(vmem_limit_bytes=VMEM),
        cost_estimate=pl.CostEstimate(flops=4 * MIB, bytes_accessed=6 * MIB, transcendentals=0),
        name="return_part",
    )(targets, received, base)


def shifted(block, tiles, cams, tile_step, cam_step):
    pairs = []
    for t in range(tiles):
        for c in range(cams):
            strip = (t + 1) % STRIPS + tile_step
            cam = c + cam_step
            if 0 <= strip < STRIPS and 0 <= cam < cams:
                pairs.append((t * cams + c, (t + tile_step) % tiles * cams + cam))
    return lax.ppermute(block, ("tile", "cam"), pairs)


def per_device(
    pixels,
    pixel_hidden,
    pixel_upstream,
    points,
    point_hidden,
    point_upstream,
    mixing,
    neighbors,
    send_list,
    pixel_weight,
    point_weight,
    kernel,
):
    tiles = lax.axis_size("tile")
    cams = lax.axis_size("cam")
    devices = tiles * cams
    slots = devices * CAP
    targets = send_list.reshape(-1)
    reads = neighbors.reshape(-1)
    blocks = (BLK_DEV, BS, C)
    outgoing, point_slope = pack(
        targets,
        points.reshape(blocks),
        point_hidden.reshape(blocks),
        point_upstream.reshape(blocks),
        devices,
    )
    outgoing, reads = lax.optimization_barrier((outgoing, reads))
    incoming = lax.all_to_all(
        outgoing, ("tile", "cam"), split_axis=0, concat_axis=0, tiled=True
    )
    pixel_slope, mixed, sums, first, last = pixel_part(
        reads, pixel_hidden, pixel_upstream, mixing, pixel_weight, slots
    )
    move = functools.partial(shifted, tiles=tiles, cams=cams)
    rim_left = jnp.concatenate(
        [
            move(last[-1:], tile_step=1, cam_step=1),
            move(last, tile_step=1, cam_step=0),
            move(last[:1], tile_step=1, cam_step=-1),
        ],
        axis=0,
    )
    rim_right = jnp.concatenate(
        [
            move(first[-1:], tile_step=-1, cam_step=1),
            move(first, tile_step=-1, cam_step=0),
            move(first[:1], tile_step=-1, cam_step=-1),
        ],
        axis=0,
    )
    padded = jnp.concatenate(
        [
            move(pixel_slope[-1:], tile_step=0, cam_step=1),
            pixel_slope,
            move(pixel_slope[:1], tile_step=0, cam_step=-1),
        ],
        axis=0,
    )
    sums, incoming, rim_left, rim_right, padded = lax.optimization_barrier(
        (sums, incoming, rim_left, rim_right, padded)
    )
    received = lax.all_to_all(
        sums.reshape(devices, CAP, BS, C),
        ("tile", "cam"),
        split_axis=0,
        concat_axis=0,
        tiled=True,
    )
    mixing_gradient, pixel_gradient = main_part(
        reads, incoming, mixed, pixels, mixing, pixel_upstream, padded, rim_left, rim_right, kernel
    )
    base = point_upstream.astype(jnp.float32) + jnp.dot(
        point_slope.reshape(BLK_DEV * BS, C), point_weight.T, preferred_element_type=jnp.float32
    )
    base, pixel_gradient = lax.optimization_barrier((base, pixel_gradient))
    point_gradient = return_part(targets, received, base.reshape(blocks))
    return (pixel_gradient, point_gradient.reshape(BLK_DEV * BS, C), mixing_gradient)


def solution(mesh):
    return jax.shard_map(
        per_device,
        mesh=mesh,
        in_specs=(
            P("cam", "tile", None),
            P("cam", "tile", None),
            P("cam", "tile", None),
            P(("tile", "cam"), None),
            P(("tile", "cam"), None),
            P(("tile", "cam"), None),
            P(("tile", "cam"), None, None),
            P(("tile", "cam"), None),
            P(("tile", "cam"), None, None),
            P(),
            P(),
            P(),
        ),
        out_specs=(
            P("cam", "tile", None),
            P(("tile", "cam"), None),
            P(("tile", "cam"), None, None),
        ),
        check_vma=False,
    )
```

```python
import functools

import jax
import jax.numpy as jnp
from jax import lax
from jax.experimental import pallas as pl
from jax.experimental.pallas import tpu as pltpu
from jax.sharding import PartitionSpec as P

C = 128
ROWS_DEV = 64
COLS_DEV = 128
K = 6
BS = 64
CAP = 2
BLK_DEV = 32
PB = 32
PIXB = 256
STRIPS = 4
MIB = 1024 * 1024
VMEM = 60 * MIB
DESTS = 16
OWNERS = 16
SPREAD = 4


def slope_of(upstream, hidden):
    argument = hidden.astype(jnp.float32)
    logistic = 0.5 + 0.5 * jnp.tanh(0.5 * argument)
    slope = logistic * (1.0 + argument * (1.0 - logistic))
    return (upstream.astype(jnp.float32) * slope).astype(jnp.bfloat16)


def pack_kernel(targets, points, hidden, upstream, out, slope_out, slope):
    step = pl.program_id(0)
    half = pl.num_programs(0) // 2
    count = hidden.shape[0]

    def fill(source, first):
        for d in range(DESTS):
            for s in range(CAP):
                out[d, s] = source[targets[0, s, first + d]]

    @pl.when(step < half)
    def _():
        values = slope_of(upstream[...], hidden[...])
        slope[pl.ds(step * count, count)] = values
        slope_out[...] = values
        fill(points, step * DESTS)

    @pl.when(step >= half)
    def _():
        fill(slope, (step - half) * DESTS)


def pack(targets, points, hidden, upstream, devices):
    half = devices // DESTS
    count = BLK_DEV // half
    part = pl.BlockSpec((count, BS, C), lambda i, t: (jnp.minimum(i, half - 1), 0, 0))
    return pl.pallas_call(
        pack_kernel,
        grid_spec=pltpu.PrefetchScalarGridSpec(
            num_scalar_prefetch=1,
            grid=(2 * half,),
            in_specs=[pl.BlockSpec((BLK_DEV, BS, C), lambda i, t: (0, 0, 0)), part, part],
            out_specs=[
                pl.BlockSpec((DESTS, CAP, BS, C), lambda i, t: (i % half, i // half, 0, 0)),
                part,
            ],
            scratch_shapes=[pltpu.VMEM((BLK_DEV, BS, C), jnp.bfloat16)],
        ),
        out_shape=[
            jax.ShapeDtypeStruct((devices, 2 * CAP, BS, C), jnp.bfloat16),
            jax.ShapeDtypeStruct((BLK_DEV, BS, C), jnp.bfloat16),
        ],
        compiler_params=pltpu.CompilerParams(vmem_limit_bytes=VMEM),
        cost_estimate=pl.CostEstimate(flops=10 * MIB, bytes_accessed=12 * MIB, transcendentals=0),
        name="pack",
    )(targets, points, hidden, upstream)


def pixel_kernel(
    neighbors, hidden, upstream, mixing, weight, slope, mixed, sums, first, last, total
):
    q = pl.program_id(0)

    @pl.when(q == 0)
    def _():
        total[...] = jnp.zeros_like(total)

    values = slope_of(upstream[...], hidden[...])
    slope[...] = values
    wide = values.astype(jnp.float32)
    for r in range(2):
        first[pl.ds(2 * q + r, 1), :] = wide[r, 0:1, :]
        last[pl.ds(2 * q + r, 1), :] = wide[r, COLS_DEV - 1 : COLS_DEV, :]
    projected = lax.dot_general(
        values.reshape(PIXB, C),
        weight[...],
        (((1,), (1,)), ((), ())),
        preferred_element_type=jnp.float32,
    ).astype(jnp.bfloat16)
    mixed[0] = projected
    term = lax.dot_general(
        mixing[0], projected, (((0,), (0,)), ((), ())), preferred_element_type=jnp.float32
    )
    for k in range(K):
        slot = neighbors[k, q]
        total[slot] += term[k * BS : (k + 1) * BS]

    @pl.when(q == PB - 1)
    def _():
        def body(i, carry):
            sums[i] = total[i].astype(jnp.bfloat16)
            return carry

        lax.fori_loop(0, total.shape[0], body, 0)


def pixel_part(neighbors, hidden, upstream, mixing, weight, slots):
    rows = pl.BlockSpec((2, COLS_DEV, C), lambda q, n: (q, 0, 0))
    return pl.pallas_call(
        pixel_kernel,
        grid_spec=pltpu.PrefetchScalarGridSpec(
            num_scalar_prefetch=1,
            grid=(PB,),
            in_specs=[
                rows,
                rows,
                pl.BlockSpec((1, PIXB, K * BS), lambda q, n: (q, 0, 0)),
                pl.BlockSpec((C, C), lambda q, n: (0, 0)),
            ],
            out_specs=[
                rows,
                pl.BlockSpec((1, PIXB, C), lambda q, n: (q, 0, 0)),
                pl.BlockSpec((slots, BS, C), lambda q, n: (0, 0, 0)),
                pl.BlockSpec((ROWS_DEV, C), lambda q, n: (0, 0)),
                pl.BlockSpec((ROWS_DEV, C), lambda q, n: (0, 0)),
            ],
            scratch_shapes=[pltpu.VMEM((slots, BS, C), jnp.float32)],
        ),
        out_shape=[
            jax.ShapeDtypeStruct((ROWS_DEV, COLS_DEV, C), jnp.bfloat16),
            jax.ShapeDtypeStruct((PB, PIXB, C), jnp.bfloat16),
            jax.ShapeDtypeStruct((slots, BS, C), jnp.bfloat16),
            jax.ShapeDtypeStruct((ROWS_DEV, C), jnp.float32),
            jax.ShapeDtypeStruct((ROWS_DEV, C), jnp.float32),
        ],
        compiler_params=pltpu.CompilerParams(vmem_limit_bytes=VMEM),
        cost_estimate=pl.CostEstimate(
            flops=1200 * MIB, bytes_accessed=18 * MIB, transcendentals=MIB
        ),
        name="pixel_part",
    )(neighbors, hidden, upstream, mixing, weight)


def main_kernel(
    neighbors, incoming, mixed, pixels, mixing, upstream, padded, left, right, kernel,
    mixing_gradient, pixel_gradient, left_side, right_side,
):
    q = pl.program_id(0)
    for k in range(K):
        slot = neighbors[k, q]
        owner = lax.div(slot, CAP)
        place = lax.rem(slot, CAP)
        right_side[k * BS : (k + 1) * BS, 0:C] = incoming[owner, place]
        right_side[k * BS : (k + 1) * BS, C : 2 * C] = incoming[owner, CAP + place]
    left_side[:, 0:C] = mixed[0]
    left_side[:, C : 2 * C] = pixels[...].reshape(PIXB, C)
    mixing_gradient[0] = lax.dot_general(
        left_side[...],
        right_side[...],
        (((1,), (1,)), ((), ())),
        preferred_element_type=jnp.float32,
    ).astype(jnp.bfloat16)
    term = jnp.dot(mixing[0], right_side[:, C : 2 * C], preferred_element_type=jnp.float32)
    column = lax.broadcasted_iota(jnp.int32, (COLS_DEV, C), 0)
    for r in range(2):
        row = 2 * q + r
        total = upstream[r].astype(jnp.float32) + term[r * COLS_DEV : (r + 1) * COLS_DEV]
        sides = []
        for e in range(3):
            part = None
            edge = None
            for a in range(3):
                gain = kernel[a, e : e + 1, :]
                piece = padded[row + 2 - a].astype(jnp.float32) * gain
                part = piece if part is None else part + piece
                if e != 1:
                    rim = right if e == 0 else left
                    corner = rim[pl.ds(row + 2 - a, 1), :] * gain
                    edge = corner if edge is None else edge + corner
            sides.append((part, edge))
        total = total + sides[1][0]
        ahead = pltpu.roll(sides[0][0], COLS_DEV - 1, 0)
        total = total + jnp.where(column == COLS_DEV - 1, sides[0][1], ahead)
        behind = pltpu.roll(sides[2][0], 1, 0)
        total = total + jnp.where(column == 0, sides[2][1], behind)
        pixel_gradient[r] = total.astype(jnp.bfloat16)


def main_part(neighbors, incoming, mixed, pixels, mixing, upstream, padded, left, right, kernel):
    rows = pl.BlockSpec((2, COLS_DEV, C), lambda q, n: (q, 0, 0))
    once = pl.Buffered(1)
    return pl.pallas_call(
        main_kernel,
        grid_spec=pltpu.PrefetchScalarGridSpec(
            num_scalar_prefetch=1,
            grid=(PB,),
            in_specs=[
                pl.BlockSpec(incoming.shape, lambda q, n: (0, 0, 0, 0), pipeline_mode=once),
                pl.BlockSpec((1, PIXB, C), lambda q, n: (q, 0, 0)),
                rows,
                pl.BlockSpec((1, PIXB, K * BS), lambda q, n: (q, 0, 0)),
                rows,
                pl.BlockSpec(padded.shape, lambda q, n: (0, 0, 0), pipeline_mode=once),
                pl.BlockSpec(left.shape, lambda q, n: (0, 0)),
                pl.BlockSpec(right.shape, lambda q, n: (0, 0)),
                pl.BlockSpec((3, 3, C), lambda q, n: (0, 0, 0)),
            ],
            out_specs=[
                pl.BlockSpec((1, PIXB, K * BS), lambda q, n: (q, 0, 0)),
                rows,
            ],
            scratch_shapes=[
                pltpu.VMEM((PIXB, 2 * C), jnp.bfloat16),
                pltpu.VMEM((K * BS, 2 * C), jnp.bfloat16),
            ],
        ),
        out_shape=[
            jax.ShapeDtypeStruct((PB, PIXB, K * BS), jnp.bfloat16),
            jax.ShapeDtypeStruct((ROWS_DEV, COLS_DEV, C), jnp.bfloat16),
        ],
        compiler_params=pltpu.CompilerParams(vmem_limit_bytes=VMEM),
        cost_estimate=pl.CostEstimate(
            flops=2600 * MIB, bytes_accessed=30 * MIB, transcendentals=0
        ),
        name="main_part",
    )(neighbors, incoming, mixed, pixels, mixing, upstream, padded, left, right, kernel)


def return_kernel(targets, received, base, out, *totals):
    step = pl.program_id(0)

    @pl.when(step == 0)
    def _():
        totals[0][...] = base[...]
        for total in totals[1:]:
            total[...] = jnp.zeros_like(total)

    for o in range(OWNERS):
        for s in range(CAP):
            block = targets[0, s, step * OWNERS + o]
            totals[(o * CAP + s) % SPREAD][block] += received[o, s].astype(jnp.float32)

    @pl.when(step == pl.num_programs(0) - 1)
    def _():
        whole = totals[0][...]
        for total in totals[1:]:
            whole = whole + total[...]
        out[...] = whole.astype(jnp.bfloat16)


def return_part(targets, received, base):
    devices = received.shape[0]
    whole = pl.BlockSpec((BLK_DEV, BS, C), lambda i, t: (0, 0, 0))
    return pl.pallas_call(
        return_kernel,
        grid_spec=pltpu.PrefetchScalarGridSpec(
            num_scalar_prefetch=1,
            grid=(devices // OWNERS,),
            in_specs=[
                pl.BlockSpec((OWNERS, CAP, BS, C), lambda i, t: (i, 0, 0, 0)),
                whole,
            ],
            out_specs=whole,
            scratch_shapes=[pltpu.VMEM((BLK_DEV, BS, C), jnp.float32)] * SPREAD,
        ),
        out_shape=jax.ShapeDtypeStruct((BLK_DEV, BS, C), jnp.bfloat16),
        compiler_params=pltpu.CompilerParams(vmem_limit_bytes=VMEM),
        cost_estimate=pl.CostEstimate(flops=4 * MIB, bytes_accessed=6 * MIB, transcendentals=0),
        name="return_part",
    )(targets, received, base)


def shifted(block, tiles, cams, tile_step, cam_step):
    pairs = []
    for t in range(tiles):
        for c in range(cams):
            strip = (t + 1) % STRIPS + tile_step
            cam = c + cam_step
            if 0 <= strip < STRIPS and 0 <= cam < cams:
                pairs.append((t * cams + c, (t + tile_step) % tiles * cams + cam))
    return lax.ppermute(block, ("tile", "cam"), pairs)


def per_device(
    pixels,
    pixel_hidden,
    pixel_upstream,
    points,
    point_hidden,
    point_upstream,
    mixing,
    neighbors,
    send_list,
    pixel_weight,
    point_weight,
    kernel,
):
    tiles = lax.axis_size("tile")
    cams = lax.axis_size("cam")
    devices = tiles * cams
    slots = devices * CAP
    targets = jnp.transpose(send_list, (0, 2, 1))
    reads = neighbors.T
    blocks = (BLK_DEV, BS, C)
    move = functools.partial(shifted, tiles=tiles, cams=cams)
    above = move(slope_of(pixel_upstream[-1:], pixel_hidden[-1:]), tile_step=0, cam_step=1)
    below = move(slope_of(pixel_upstream[:1], pixel_hidden[:1]), tile_step=0, cam_step=-1)
    outgoing, point_slope = pack(
        targets,
        points.reshape(blocks),
        point_hidden.reshape(blocks),
        point_upstream.reshape(blocks),
        devices,
    )
    outgoing, reads, above, below = lax.optimization_barrier((outgoing, reads, above, below))
    incoming = lax.all_to_all(
        outgoing, ("tile", "cam"), split_axis=0, concat_axis=0, tiled=True
    )
    pixel_slope, mixed, sums, first, last = pixel_part(
        reads, pixel_hidden, pixel_upstream, mixing, pixel_weight, slots
    )
    padded = jnp.concatenate([above, pixel_slope, below], axis=0)
    first = jnp.concatenate(
        [above[:, 0].astype(jnp.float32), first, below[:, 0].astype(jnp.float32)], axis=0
    )
    last = jnp.concatenate(
        [above[:, -1].astype(jnp.float32), last, below[:, -1].astype(jnp.float32)], axis=0
    )
    rim_left = move(last, tile_step=1, cam_step=0)
    rim_right = move(first, tile_step=-1, cam_step=0)
    sums, incoming, rim_left, rim_right, padded = lax.optimization_barrier(
        (sums, incoming, rim_left, rim_right, padded)
    )
    received = lax.all_to_all(
        sums.reshape(devices, CAP, BS, C),
        ("tile", "cam"),
        split_axis=0,
        concat_axis=0,
        tiled=True,
    )
    mixing_gradient, pixel_gradient = main_part(
        reads, incoming, mixed, pixels, mixing, pixel_upstream, padded, rim_left, rim_right, kernel
    )
    base = point_upstream.astype(jnp.float32) + jnp.dot(
        point_slope.reshape(BLK_DEV * BS, C), point_weight.T, preferred_element_type=jnp.float32
    )
    base, pixel_gradient = lax.optimization_barrier((base, pixel_gradient))
    point_gradient = return_part(targets, received, base.reshape(blocks))
    return (pixel_gradient, point_gradient.reshape(BLK_DEV * BS, C), mixing_gradient)


def solution(mesh):
    return jax.shard_map(
        per_device,
        mesh=mesh,
        in_specs=(
            P("cam", "tile", None),
            P("cam", "tile", None),
            P("cam", "tile", None),
            P(("tile", "cam"), None),
            P(("tile", "cam"), None),
            P(("tile", "cam"), None),
            P(("tile", "cam"), None, None),
            P(("tile", "cam"), None),
            P(("tile", "cam"), None, None),
            P(),
            P(),
            P(),
        ),
        out_specs=(
            P("cam", "tile", None),
            P(("tile", "cam"), None),
            P(("tile", "cam"), None, None),
        ),
        check_vma=False,
    )
```

```python
import functools

import jax
import jax.numpy as jnp
from jax import lax
from jax.experimental import pallas as pl
from jax.experimental.pallas import tpu as pltpu
from jax.sharding import PartitionSpec as P

C = 128
ROWS_DEV = 64
COLS_DEV = 128
K = 6
BS = 64
CAP = 2
BLK_DEV = 32
PB = 32
PIXB = 256
STRIPS = 4
MIB = 1024 * 1024
VMEM = 60 * MIB
DESTS = 4
OWNERS = 16
SPREAD = 4


def slope_of(upstream, hidden):
    argument = hidden.astype(jnp.float32)
    logistic = 0.5 + 0.5 * jnp.tanh(0.5 * argument)
    slope = logistic * (1.0 + argument * (1.0 - logistic))
    return (upstream.astype(jnp.float32) * slope).astype(jnp.bfloat16)


def pack_kernel(targets, points, hidden, upstream, out, slope, sem):
    def send(source, first):
        def body(i, carry):
            for j in range(DESTS):
                d = i * DESTS + j
                for s in range(CAP):
                    block = source.at[targets[0, s, d]]
                    pltpu.make_async_copy(block, out.at[d, first + s], sem).start()
            return carry

        lax.fori_loop(0, out.shape[0] // DESTS, body, 0)

    def fill(i, carry):
        part = pl.ds(2 * i, 2)
        slope[part] = slope_of(upstream[part], hidden[part])
        return carry

    send(points, 0)
    lax.fori_loop(0, BLK_DEV // 2, fill, 0)
    send(slope, CAP)
    pltpu.make_async_copy(out, out, sem).wait()


def pack(targets, points, hidden, upstream, devices):
    whole = pl.BlockSpec(memory_space=pltpu.VMEM)
    return pl.pallas_call(
        pack_kernel,
        in_specs=[pl.BlockSpec(memory_space=pltpu.SMEM), whole, whole, whole],
        out_specs=[pl.BlockSpec(memory_space=pl.ANY), whole],
        out_shape=[
            jax.ShapeDtypeStruct((devices, 2 * CAP, BS, C), jnp.bfloat16),
            jax.ShapeDtypeStruct((BLK_DEV, BS, C), jnp.bfloat16),
        ],
        scratch_shapes=[pltpu.SemaphoreType.DMA(())],
        compiler_params=pltpu.CompilerParams(vmem_limit_bytes=VMEM),
        cost_estimate=pl.CostEstimate(flops=10 * MIB, bytes_accessed=12 * MIB, transcendentals=0),
        name="pack",
    )(targets, points, hidden, upstream)


def pixel_kernel(
    neighbors, hidden, upstream, mixing, weight, slope, mixed, sums, first, last, total
):
    q = pl.program_id(0)

    @pl.when(q == 0)
    def _():
        total[...] = jnp.zeros_like(total)

    values = slope_of(upstream[...], hidden[...])
    slope[...] = values
    wide = values.astype(jnp.float32)
    for r in range(2):
        first[pl.ds(2 * q + r, 1), :] = wide[r, 0:1, :]
        last[pl.ds(2 * q + r, 1), :] = wide[r, COLS_DEV - 1 : COLS_DEV, :]
    projected = lax.dot_general(
        values.reshape(PIXB, C),
        weight[...],
        (((1,), (1,)), ((), ())),
        preferred_element_type=jnp.float32,
    ).astype(jnp.bfloat16)
    mixed[0] = projected
    term = lax.dot_general(
        mixing[0], projected, (((0,), (0,)), ((), ())), preferred_element_type=jnp.float32
    )
    for k in range(K):
        slot = neighbors[k, q]
        total[slot] += term[k * BS : (k + 1) * BS]

    @pl.when(q == PB - 1)
    def _():
        def body(i, carry):
            sums[i] = total[i].astype(jnp.bfloat16)
            return carry

        lax.fori_loop(0, total.shape[0], body, 0)


def pixel_part(neighbors, hidden, upstream, mixing, weight, slots):
    rows = pl.BlockSpec((2, COLS_DEV, C), lambda q, n: (q, 0, 0))
    return pl.pallas_call(
        pixel_kernel,
        grid_spec=pltpu.PrefetchScalarGridSpec(
            num_scalar_prefetch=1,
            grid=(PB,),
            in_specs=[
                rows,
                rows,
                pl.BlockSpec((1, PIXB, K * BS), lambda q, n: (q, 0, 0)),
                pl.BlockSpec((C, C), lambda q, n: (0, 0)),
            ],
            out_specs=[
                rows,
                pl.BlockSpec((1, PIXB, C), lambda q, n: (q, 0, 0)),
                pl.BlockSpec((slots, BS, C), lambda q, n: (0, 0, 0)),
                pl.BlockSpec((ROWS_DEV, C), lambda q, n: (0, 0)),
                pl.BlockSpec((ROWS_DEV, C), lambda q, n: (0, 0)),
            ],
            scratch_shapes=[pltpu.VMEM((slots, BS, C), jnp.float32)],
        ),
        out_shape=[
            jax.ShapeDtypeStruct((ROWS_DEV, COLS_DEV, C), jnp.bfloat16),
            jax.ShapeDtypeStruct((PB, PIXB, C), jnp.bfloat16),
            jax.ShapeDtypeStruct((slots, BS, C), jnp.bfloat16),
            jax.ShapeDtypeStruct((ROWS_DEV, C), jnp.float32),
            jax.ShapeDtypeStruct((ROWS_DEV, C), jnp.float32),
        ],
        compiler_params=pltpu.CompilerParams(vmem_limit_bytes=VMEM),
        cost_estimate=pl.CostEstimate(
            flops=1200 * MIB, bytes_accessed=18 * MIB, transcendentals=MIB
        ),
        name="pixel_part",
    )(neighbors, hidden, upstream, mixing, weight)


def main_kernel(
    neighbors, incoming, mixed, pixels, mixing, upstream, padded, left, right, kernel,
    mixing_gradient, pixel_gradient, left_side, right_side,
):
    q = pl.program_id(0)
    for k in range(K):
        slot = neighbors[k, q]
        owner = lax.div(slot, CAP)
        place = lax.rem(slot, CAP)
        right_side[k * BS : (k + 1) * BS, 0:C] = incoming[owner, place]
        right_side[k * BS : (k + 1) * BS, C : 2 * C] = incoming[owner, CAP + place]
    left_side[:, 0:C] = mixed[0]
    left_side[:, C : 2 * C] = pixels[...].reshape(PIXB, C)
    mixing_gradient[0] = lax.dot_general(
        left_side[...],
        right_side[...],
        (((1,), (1,)), ((), ())),
        preferred_element_type=jnp.float32,
    ).astype(jnp.bfloat16)
    term = jnp.dot(mixing[0], right_side[:, C : 2 * C], preferred_element_type=jnp.float32)
    column = lax.broadcasted_iota(jnp.int32, (COLS_DEV, C), 0)
    for r in range(2):
        row = 2 * q + r
        total = upstream[r].astype(jnp.float32) + term[r * COLS_DEV : (r + 1) * COLS_DEV]
        sides = []
        for e in range(3):
            part = None
            edge = None
            for a in range(3):
                gain = kernel[a, e : e + 1, :]
                piece = padded[row + 2 - a].astype(jnp.float32) * gain
                part = piece if part is None else part + piece
                if e != 1:
                    rim = right if e == 0 else left
                    corner = rim[pl.ds(row + 2 - a, 1), :] * gain
                    edge = corner if edge is None else edge + corner
            sides.append((part, edge))
        total = total + sides[1][0]
        ahead = pltpu.roll(sides[0][0], COLS_DEV - 1, 0)
        total = total + jnp.where(column == COLS_DEV - 1, sides[0][1], ahead)
        behind = pltpu.roll(sides[2][0], 1, 0)
        total = total + jnp.where(column == 0, sides[2][1], behind)
        pixel_gradient[r] = total.astype(jnp.bfloat16)


def main_part(neighbors, incoming, mixed, pixels, mixing, upstream, padded, left, right, kernel):
    rows = pl.BlockSpec((2, COLS_DEV, C), lambda q, n: (q, 0, 0))
    once = pl.Buffered(1)
    return pl.pallas_call(
        main_kernel,
        grid_spec=pltpu.PrefetchScalarGridSpec(
            num_scalar_prefetch=1,
            grid=(PB,),
            in_specs=[
                pl.BlockSpec(incoming.shape, lambda q, n: (0, 0, 0, 0), pipeline_mode=once),
                pl.BlockSpec((1, PIXB, C), lambda q, n: (q, 0, 0)),
                rows,
                pl.BlockSpec((1, PIXB, K * BS), lambda q, n: (q, 0, 0)),
                rows,
                pl.BlockSpec(padded.shape, lambda q, n: (0, 0, 0), pipeline_mode=once),
                pl.BlockSpec(left.shape, lambda q, n: (0, 0)),
                pl.BlockSpec(right.shape, lambda q, n: (0, 0)),
                pl.BlockSpec((3, 3, C), lambda q, n: (0, 0, 0)),
            ],
            out_specs=[
                pl.BlockSpec((1, PIXB, K * BS), lambda q, n: (q, 0, 0)),
                rows,
            ],
            scratch_shapes=[
                pltpu.VMEM((PIXB, 2 * C), jnp.bfloat16),
                pltpu.VMEM((K * BS, 2 * C), jnp.bfloat16),
            ],
        ),
        out_shape=[
            jax.ShapeDtypeStruct((PB, PIXB, K * BS), jnp.bfloat16),
            jax.ShapeDtypeStruct((ROWS_DEV, COLS_DEV, C), jnp.bfloat16),
        ],
        compiler_params=pltpu.CompilerParams(vmem_limit_bytes=VMEM),
        cost_estimate=pl.CostEstimate(
            flops=2600 * MIB, bytes_accessed=30 * MIB, transcendentals=0
        ),
        name="main_part",
    )(neighbors, incoming, mixed, pixels, mixing, upstream, padded, left, right, kernel)


def return_kernel(targets, received, base, out, landed, sems, *totals):
    parts = received.shape[0] // OWNERS

    def fetch(i):
        part = pl.ds(i * OWNERS, OWNERS)
        return pltpu.make_async_copy(received.at[part], landed.at[part], sems.at[i])

    for i in range(parts):
        fetch(i).start()
    totals[0][...] = base[...]
    for total in totals[1:]:
        total[...] = jnp.zeros_like(total)

    def body(i, carry):
        fetch(i).wait()
        for j in range(OWNERS):
            for s in range(CAP):
                o = i * OWNERS + j
                block = targets[0, s, o]
                totals[(j * CAP + s) % SPREAD][block] += landed[o, s].astype(jnp.float32)
        return carry

    lax.fori_loop(0, parts, body, 0)
    whole = totals[0][...]
    for total in totals[1:]:
        whole = whole + total[...]
    out[...] = whole.astype(jnp.bfloat16)


def return_part(targets, received, base):
    whole = pl.BlockSpec(memory_space=pltpu.VMEM)
    return pl.pallas_call(
        return_kernel,
        in_specs=[
            pl.BlockSpec(memory_space=pltpu.SMEM),
            pl.BlockSpec(memory_space=pl.ANY),
            whole,
        ],
        out_specs=whole,
        scratch_shapes=[
            pltpu.VMEM(received.shape, jnp.bfloat16),
            pltpu.SemaphoreType.DMA((received.shape[0] // OWNERS,)),
        ]
        + [pltpu.VMEM((BLK_DEV, BS, C), jnp.float32)] * SPREAD,
        out_shape=jax.ShapeDtypeStruct((BLK_DEV, BS, C), jnp.bfloat16),
        compiler_params=pltpu.CompilerParams(vmem_limit_bytes=VMEM),
        cost_estimate=pl.CostEstimate(flops=4 * MIB, bytes_accessed=6 * MIB, transcendentals=0),
        name="return_part",
    )(targets, received, base)


def shifted(block, tiles, cams, tile_step, cam_step):
    pairs = []
    for t in range(tiles):
        for c in range(cams):
            strip = (t + 1) % STRIPS + tile_step
            cam = c + cam_step
            if 0 <= strip < STRIPS and 0 <= cam < cams:
                pairs.append((t * cams + c, (t + tile_step) % tiles * cams + cam))
    return lax.ppermute(block, ("tile", "cam"), pairs)


def per_device(
    pixels,
    pixel_hidden,
    pixel_upstream,
    points,
    point_hidden,
    point_upstream,
    mixing,
    neighbors,
    send_list,
    pixel_weight,
    point_weight,
    kernel,
):
    tiles = lax.axis_size("tile")
    cams = lax.axis_size("cam")
    devices = tiles * cams
    slots = devices * CAP
    targets = jnp.transpose(send_list, (0, 2, 1))
    reads = neighbors.T
    blocks = (BLK_DEV, BS, C)
    move = functools.partial(shifted, tiles=tiles, cams=cams)
    above = move(slope_of(pixel_upstream[-1:], pixel_hidden[-1:]), tile_step=0, cam_step=1)
    below = move(slope_of(pixel_upstream[:1], pixel_hidden[:1]), tile_step=0, cam_step=-1)
    outgoing, point_slope = pack(
        targets,
        points.reshape(blocks),
        point_hidden.reshape(blocks),
        point_upstream.reshape(blocks),
        devices,
    )
    outgoing, reads, above, below = lax.optimization_barrier((outgoing, reads, above, below))
    incoming = lax.all_to_all(
        outgoing, ("tile", "cam"), split_axis=0, concat_axis=0, tiled=True
    )
    pixel_slope, mixed, sums, first, last = pixel_part(
        reads, pixel_hidden, pixel_upstream, mixing, pixel_weight, slots
    )
    padded = jnp.concatenate([above, pixel_slope, below], axis=0)
    first = jnp.concatenate(
        [above[:, 0].astype(jnp.float32), first, below[:, 0].astype(jnp.float32)], axis=0
    )
    last = jnp.concatenate(
        [above[:, -1].astype(jnp.float32), last, below[:, -1].astype(jnp.float32)], axis=0
    )
    rim_left = move(last, tile_step=1, cam_step=0)
    rim_right = move(first, tile_step=-1, cam_step=0)
    sums, incoming, rim_left, rim_right, padded = lax.optimization_barrier(
        (sums, incoming, rim_left, rim_right, padded)
    )
    received = lax.all_to_all(
        sums.reshape(devices, CAP, BS, C),
        ("tile", "cam"),
        split_axis=0,
        concat_axis=0,
        tiled=True,
    )
    mixing_gradient, pixel_gradient = main_part(
        reads, incoming, mixed, pixels, mixing, pixel_upstream, padded, rim_left, rim_right, kernel
    )
    base = point_upstream.astype(jnp.float32) + jnp.dot(
        point_slope.reshape(BLK_DEV * BS, C), point_weight.T, preferred_element_type=jnp.float32
    )
    base, pixel_gradient = lax.optimization_barrier((base, pixel_gradient))
    point_gradient = return_part(targets, received, base.reshape(blocks))
    return (pixel_gradient, point_gradient.reshape(BLK_DEV * BS, C), mixing_gradient)


def solution(mesh):
    return jax.shard_map(
        per_device,
        mesh=mesh,
        in_specs=(
            P("cam", "tile", None),
            P("cam", "tile", None),
            P("cam", "tile", None),
            P(("tile", "cam"), None),
            P(("tile", "cam"), None),
            P(("tile", "cam"), None),
            P(("tile", "cam"), None, None),
            P(("tile", "cam"), None),
            P(("tile", "cam"), None, None),
            P(),
            P(),
            P(),
        ),
        out_specs=(
            P("cam", "tile", None),
            P(("tile", "cam"), None),
            P(("tile", "cam"), None, None),
        ),
        check_vma=False,
    )
```

```python
import functools

import jax
import jax.numpy as jnp
from jax import lax
from jax.experimental import pallas as pl
from jax.experimental.pallas import tpu as pltpu
from jax.sharding import PartitionSpec as P

C = 128
ROWS_DEV = 64
COLS_DEV = 128
K = 6
BS = 64
CAP = 2
BLK_DEV = 32
PB = 32
PIXB = 256
STRIPS = 4
MIB = 1024 * 1024
VMEM = 60 * MIB
DESTS = 4
OWNERS = 16
SPREAD = 4


def slope_of(upstream, hidden):
    argument = hidden.astype(jnp.float32)
    logistic = 0.5 + 0.5 * jnp.tanh(0.5 * argument)
    slope = logistic * (1.0 + argument * (1.0 - logistic))
    return (upstream.astype(jnp.float32) * slope).astype(jnp.bfloat16)


def pack_kernel(targets, points, hidden, upstream, out, slope, sem):
    def send(source, first):
        def body(i, carry):
            for j in range(DESTS):
                d = i * DESTS + j
                for s in range(CAP):
                    block = source.at[targets[0, s, d]]
                    pltpu.make_async_copy(block, out.at[d, first + s], sem).start()
            return carry

        lax.fori_loop(0, out.shape[0] // DESTS, body, 0)

    def fill(i, carry):
        part = pl.ds(2 * i, 2)
        slope[part] = slope_of(upstream[part], hidden[part])
        return carry

    send(points, 0)
    lax.fori_loop(0, BLK_DEV // 2, fill, 0)
    send(slope, CAP)
    pltpu.make_async_copy(out, out, sem).wait()


def pack(targets, points, hidden, upstream, devices):
    whole = pl.BlockSpec(memory_space=pltpu.VMEM)
    return pl.pallas_call(
        pack_kernel,
        in_specs=[pl.BlockSpec(memory_space=pltpu.SMEM), whole, whole, whole],
        out_specs=[pl.BlockSpec(memory_space=pl.ANY), whole],
        out_shape=[
            jax.ShapeDtypeStruct((devices, 2 * CAP, BS, C), jnp.bfloat16),
            jax.ShapeDtypeStruct((BLK_DEV, BS, C), jnp.bfloat16),
        ],
        scratch_shapes=[pltpu.SemaphoreType.DMA(())],
        compiler_params=pltpu.CompilerParams(vmem_limit_bytes=VMEM),
        cost_estimate=pl.CostEstimate(flops=10 * MIB, bytes_accessed=12 * MIB, transcendentals=0),
        name="pack",
    )(targets, points, hidden, upstream)


def pixel_kernel(
    neighbors, hidden, upstream, mixing, weight, slope, mixed, sums, first, last, total
):
    q = pl.program_id(0)

    @pl.when(q == 0)
    def _():
        total[...] = jnp.zeros_like(total)

    values = slope_of(upstream[...], hidden[...])
    slope[...] = values
    wide = values.astype(jnp.float32)
    for r in range(2):
        first[pl.ds(2 * q + r, 1), :] = wide[r, 0:1, :]
        last[pl.ds(2 * q + r, 1), :] = wide[r, COLS_DEV - 1 : COLS_DEV, :]
    projected = lax.dot_general(
        values.reshape(PIXB, C),
        weight[...],
        (((1,), (1,)), ((), ())),
        preferred_element_type=jnp.float32,
    ).astype(jnp.bfloat16)
    mixed[0] = projected
    term = lax.dot_general(
        mixing[0], projected, (((0,), (0,)), ((), ())), preferred_element_type=jnp.float32
    )
    for k in range(K):
        slot = neighbors[k, q]
        total[slot] += term[k * BS : (k + 1) * BS]

    @pl.when(q == PB - 1)
    def _():
        def body(i, carry):
            sums[i] = total[i].astype(jnp.bfloat16)
            return carry

        lax.fori_loop(0, total.shape[0], body, 0)


def pixel_part(neighbors, hidden, upstream, mixing, weight, slots):
    rows = pl.BlockSpec((2, COLS_DEV, C), lambda q, n: (q, 0, 0))
    return pl.pallas_call(
        pixel_kernel,
        grid_spec=pltpu.PrefetchScalarGridSpec(
            num_scalar_prefetch=1,
            grid=(PB,),
            in_specs=[
                rows,
                rows,
                pl.BlockSpec((1, PIXB, K * BS), lambda q, n: (q, 0, 0)),
                pl.BlockSpec((C, C), lambda q, n: (0, 0)),
            ],
            out_specs=[
                rows,
                pl.BlockSpec((1, PIXB, C), lambda q, n: (q, 0, 0)),
                pl.BlockSpec((slots, BS, C), lambda q, n: (0, 0, 0)),
                pl.BlockSpec((ROWS_DEV, C), lambda q, n: (0, 0)),
                pl.BlockSpec((ROWS_DEV, C), lambda q, n: (0, 0)),
            ],
            scratch_shapes=[pltpu.VMEM((slots, BS, C), jnp.float32)],
        ),
        out_shape=[
            jax.ShapeDtypeStruct((ROWS_DEV, COLS_DEV, C), jnp.bfloat16),
            jax.ShapeDtypeStruct((PB, PIXB, C), jnp.bfloat16),
            jax.ShapeDtypeStruct((slots, BS, C), jnp.bfloat16),
            jax.ShapeDtypeStruct((ROWS_DEV, C), jnp.float32),
            jax.ShapeDtypeStruct((ROWS_DEV, C), jnp.float32),
        ],
        compiler_params=pltpu.CompilerParams(vmem_limit_bytes=VMEM),
        cost_estimate=pl.CostEstimate(
            flops=1200 * MIB, bytes_accessed=18 * MIB, transcendentals=MIB
        ),
        name="pixel_part",
    )(neighbors, hidden, upstream, mixing, weight)


def main_kernel(
    neighbors, incoming, mixed, pixels, mixing, upstream, padded, left, right, kernel,
    mixing_gradient, pixel_gradient, totals, left_side, right_side,
):
    q = pl.program_id(0)
    for k in range(K):
        slot = neighbors[k, q]
        owner = lax.div(slot, CAP)
        place = lax.rem(slot, CAP)
        right_side[k * BS : (k + 1) * BS, 0:C] = incoming[owner, place]
        right_side[k * BS : (k + 1) * BS, C : 2 * C] = incoming[owner, CAP + place]
    left_side[:, 0:C] = mixed[0]
    left_side[:, C : 2 * C] = pixels[...].reshape(PIXB, C)
    mixing_gradient[0] = lax.dot_general(
        left_side[...],
        right_side[...],
        (((1,), (1,)), ((), ())),
        preferred_element_type=jnp.float32,
    ).astype(jnp.bfloat16)
    term = jnp.dot(mixing[0], right_side[:, C : 2 * C], preferred_element_type=jnp.float32)
    column = lax.broadcasted_iota(jnp.int32, (COLS_DEV, C), 0)
    for r in range(2):
        row = 2 * q + r
        total = upstream[r].astype(jnp.float32) + term[r * COLS_DEV : (r + 1) * COLS_DEV]
        sides = []
        for e in range(3):
            part = None
            edge = None
            for a in range(3):
                gain = kernel[a, e : e + 1, :]
                piece = padded[row + 2 - a].astype(jnp.float32) * gain
                part = piece if part is None else part + piece
                if e != 1:
                    rim = right if e == 0 else left
                    corner = rim[pl.ds(row + 2 - a, 1), :] * gain
                    edge = corner if edge is None else edge + corner
            sides.append((part, edge))
        total = total + sides[1][0]
        ahead = pltpu.roll(sides[0][0], COLS_DEV - 1, 0)
        total = total + jnp.where(column == COLS_DEV - 1, sides[0][1], ahead)
        behind = pltpu.roll(sides[2][0], 1, 0)
        total = total + jnp.where(column == 0, sides[2][1], behind)
        pixel_gradient[r] = total.astype(jnp.bfloat16)

        @pl.when(q == r * (PB - 1))
        def _():
            totals[2 * r : 2 * r + 1] = total[0:1]
            totals[2 * r + 1 : 2 * r + 2] = total[COLS_DEV - 1 : COLS_DEV]


def main_part(neighbors, incoming, mixed, pixels, mixing, upstream, padded, left, right, kernel):
    rows = pl.BlockSpec((2, COLS_DEV, C), lambda q, n: (q, 0, 0))
    once = pl.Buffered(1)
    return pl.pallas_call(
        main_kernel,
        grid_spec=pltpu.PrefetchScalarGridSpec(
            num_scalar_prefetch=1,
            grid=(PB,),
            in_specs=[
                pl.BlockSpec(incoming.shape, lambda q, n: (0, 0, 0, 0), pipeline_mode=once),
                pl.BlockSpec((1, PIXB, C), lambda q, n: (q, 0, 0)),
                rows,
                pl.BlockSpec((1, PIXB, K * BS), lambda q, n: (q, 0, 0)),
                rows,
                pl.BlockSpec(padded.shape, lambda q, n: (0, 0, 0), pipeline_mode=once),
                pl.BlockSpec(left.shape, lambda q, n: (0, 0)),
                pl.BlockSpec(right.shape, lambda q, n: (0, 0)),
                pl.BlockSpec((3, 3, C), lambda q, n: (0, 0, 0)),
            ],
            out_specs=[
                pl.BlockSpec((1, PIXB, K * BS), lambda q, n: (q, 0, 0)),
                rows,
                pl.BlockSpec((4, C), lambda q, n: (0, 0)),
            ],
            scratch_shapes=[
                pltpu.VMEM((PIXB, 2 * C), jnp.bfloat16),
                pltpu.VMEM((K * BS, 2 * C), jnp.bfloat16),
            ],
        ),
        out_shape=[
            jax.ShapeDtypeStruct((PB, PIXB, K * BS), jnp.bfloat16),
            jax.ShapeDtypeStruct((ROWS_DEV, COLS_DEV, C), jnp.bfloat16),
            jax.ShapeDtypeStruct((4, C), jnp.float32),
        ],
        compiler_params=pltpu.CompilerParams(vmem_limit_bytes=VMEM),
        cost_estimate=pl.CostEstimate(
            flops=2600 * MIB, bytes_accessed=30 * MIB, transcendentals=0
        ),
        name="main_part",
    )(neighbors, incoming, mixed, pixels, mixing, upstream, padded, left, right, kernel)


def corner_kernel(totals, gains, corners, gradient, out):
    i = pl.program_id(0)
    value = totals[pl.ds(i, 1), :] + gains[pl.ds(i, 1), :] * corners[pl.ds(i, 1), :]
    column = lax.broadcasted_iota(jnp.int32, (16, C), 0)
    block = jnp.where(column == lax.rem(i, 2) * 15, value, gradient[0].astype(jnp.float32))
    out[0] = block.astype(jnp.bfloat16)


def corner_part(totals, gains, corners, gradient):
    whole = pl.BlockSpec((4, C), lambda i: (0, 0))
    ends = ROWS_DEV - 1, COLS_DEV // 16 - 1
    block = pl.BlockSpec((1, 16, C), lambda i: (i // 2 * ends[0], i % 2 * ends[1], 0))
    return pl.pallas_call(
        corner_kernel,
        grid=(4,),
        in_specs=[whole, whole, whole, block],
        out_specs=block,
        out_shape=jax.ShapeDtypeStruct(gradient.shape, jnp.bfloat16),
        input_output_aliases={3: 0},
        compiler_params=pltpu.CompilerParams(vmem_limit_bytes=VMEM),
        cost_estimate=pl.CostEstimate(flops=4096, bytes_accessed=65536, transcendentals=0),
        name="corner_part",
    )(totals, gains, corners, gradient)


def return_kernel(targets, received, base, out, landed, sems, *totals):
    parts = received.shape[0] // OWNERS

    def fetch(i):
        part = pl.ds(i * OWNERS, OWNERS)
        return pltpu.make_async_copy(received.at[part], landed.at[part], sems.at[i])

    for i in range(parts):
        fetch(i).start()
    totals[0][...] = base[...]
    for total in totals[1:]:
        total[...] = jnp.zeros_like(total)

    def body(i, carry):
        fetch(i).wait()
        for j in range(OWNERS):
            for s in range(CAP):
                o = i * OWNERS + j
                block = targets[0, s, o]
                totals[(j * CAP + s) % SPREAD][block] += landed[o, s].astype(jnp.float32)
        return carry

    lax.fori_loop(0, parts, body, 0)
    whole = totals[0][...]
    for total in totals[1:]:
        whole = whole + total[...]
    out[...] = whole.astype(jnp.bfloat16)


def return_part(targets, received, base):
    whole = pl.BlockSpec(memory_space=pltpu.VMEM)
    return pl.pallas_call(
        return_kernel,
        in_specs=[
            pl.BlockSpec(memory_space=pltpu.SMEM),
            pl.BlockSpec(memory_space=pl.ANY),
            whole,
        ],
        out_specs=whole,
        scratch_shapes=[
            pltpu.VMEM(received.shape, jnp.bfloat16),
            pltpu.SemaphoreType.DMA((received.shape[0] // OWNERS,)),
        ]
        + [pltpu.VMEM((BLK_DEV, BS, C), jnp.float32)] * SPREAD,
        out_shape=jax.ShapeDtypeStruct((BLK_DEV, BS, C), jnp.bfloat16),
        compiler_params=pltpu.CompilerParams(vmem_limit_bytes=VMEM),
        cost_estimate=pl.CostEstimate(flops=4 * MIB, bytes_accessed=6 * MIB, transcendentals=0),
        name="return_part",
    )(targets, received, base)


def shifted(block, tiles, cams, tile_step, cam_step):
    pairs = []
    for t in range(tiles):
        for c in range(cams):
            strip = (t + 1) % STRIPS + tile_step
            cam = c + cam_step
            if 0 <= strip < STRIPS and 0 <= cam < cams:
                pairs.append((t * cams + c, (t + tile_step) % tiles * cams + cam))
    return lax.ppermute(block, ("tile", "cam"), pairs)


def per_device(
    pixels,
    pixel_hidden,
    pixel_upstream,
    points,
    point_hidden,
    point_upstream,
    mixing,
    neighbors,
    send_list,
    pixel_weight,
    point_weight,
    kernel,
):
    tiles = lax.axis_size("tile")
    cams = lax.axis_size("cam")
    devices = tiles * cams
    slots = devices * CAP
    targets = jnp.transpose(send_list, (0, 2, 1))
    reads = neighbors.T
    blocks = (BLK_DEV, BS, C)
    outgoing, point_slope = pack(
        targets,
        points.reshape(blocks),
        point_hidden.reshape(blocks),
        point_upstream.reshape(blocks),
        devices,
    )
    outgoing, reads = lax.optimization_barrier((outgoing, reads))
    incoming = lax.all_to_all(
        outgoing, ("tile", "cam"), split_axis=0, concat_axis=0, tiled=True
    )
    pixel_slope, mixed, sums, first, last = pixel_part(
        reads, pixel_hidden, pixel_upstream, mixing, pixel_weight, slots
    )
    move = functools.partial(shifted, tiles=tiles, cams=cams)
    padded = jnp.concatenate(
        [
            move(pixel_slope[-1:], tile_step=0, cam_step=1),
            pixel_slope,
            move(pixel_slope[:1], tile_step=0, cam_step=-1),
        ],
        axis=0,
    )
    edges = ((1, 1), (0, 0))
    rim_left = jnp.pad(move(last, tile_step=1, cam_step=0), edges)
    rim_right = jnp.pad(move(first, tile_step=-1, cam_step=0), edges)
    sums, incoming, rim_left, rim_right, padded, point_slope = lax.optimization_barrier(
        (sums, incoming, rim_left, rim_right, padded, point_slope)
    )
    received = lax.all_to_all(
        sums.reshape(devices, CAP, BS, C),
        ("tile", "cam"),
        split_axis=0,
        concat_axis=0,
        tiled=True,
    )
    base = point_upstream.astype(jnp.float32) + jnp.dot(
        point_slope.reshape(BLK_DEV * BS, C), point_weight.T, preferred_element_type=jnp.float32
    )
    base, first, last = lax.optimization_barrier((base, first, last))
    corners = jnp.concatenate(
        [
            move(last[-1:], tile_step=1, cam_step=1),
            move(first[-1:], tile_step=-1, cam_step=1),
            move(last[:1], tile_step=1, cam_step=-1),
            move(first[:1], tile_step=-1, cam_step=-1),
        ],
        axis=0,
    )
    mixing_gradient, pixel_gradient, totals = main_part(
        reads, incoming, mixed, pixels, mixing, pixel_upstream, padded, rim_left, rim_right, kernel
    )
    gains = jnp.stack([kernel[2, 2], kernel[2, 0], kernel[0, 2], kernel[0, 0]])
    pixel_gradient = corner_part(totals, gains, corners, pixel_gradient)
    base, pixel_gradient = lax.optimization_barrier((base, pixel_gradient))
    point_gradient = return_part(targets, received, base.reshape(blocks))
    return (pixel_gradient, point_gradient.reshape(BLK_DEV * BS, C), mixing_gradient)


def solution(mesh):
    return jax.shard_map(
        per_device,
        mesh=mesh,
        in_specs=(
            P("cam", "tile", None),
            P("cam", "tile", None),
            P("cam", "tile", None),
            P(("tile", "cam"), None),
            P(("tile", "cam"), None),
            P(("tile", "cam"), None),
            P(("tile", "cam"), None, None),
            P(("tile", "cam"), None),
            P(("tile", "cam"), None, None),
            P(),
            P(),
            P(),
        ),
        out_specs=(
            P("cam", "tile", None),
            P(("tile", "cam"), None),
            P(("tile", "cam"), None, None),
        ),
        check_vma=False,
    )
```

```python
import functools

import jax
import jax.numpy as jnp
from jax import lax
from jax.experimental import pallas as pl
from jax.experimental.pallas import tpu as pltpu
from jax.sharding import PartitionSpec as P

C = 128
ROWS_DEV = 64
COLS_DEV = 128
K = 6
BS = 64
CAP = 2
BLK_DEV = 32
PB = 32
PIXB = 256
STRIPS = 4
MIB = 1024 * 1024
VMEM = 60 * MIB
DESTS = 4
OWNERS = 16
SPREAD = 4


def slope_of(upstream, hidden):
    argument = hidden.astype(jnp.float32)
    logistic = 0.5 + 0.5 * jnp.tanh(0.5 * argument)
    slope = logistic * (1.0 + argument * (1.0 - logistic))
    return (upstream.astype(jnp.float32) * slope).astype(jnp.bfloat16)


def pack_kernel(
    targets, points_in, hidden_in, upstream_in, out, slope, points, hidden, upstream, sem, sems
):
    loads = [
        pltpu.make_async_copy(source, target, sems.at[i])
        for i, (source, target) in enumerate(
            ((points_in, points), (hidden_in, hidden), (upstream_in, upstream))
        )
    ]
    for load in loads:
        load.start()

    def send(source, first):
        def body(i, carry):
            for j in range(DESTS):
                d = i * DESTS + j
                for s in range(CAP):
                    block = source.at[targets[0, s, d]]
                    pltpu.make_async_copy(block, out.at[d, first + s], sem).start()
            return carry

        lax.fori_loop(0, out.shape[0] // DESTS, body, 0)

    def fill(i, carry):
        part = pl.ds(2 * i, 2)
        slope[part] = slope_of(upstream[part], hidden[part])
        return carry

    loads[0].wait()
    send(points, 0)
    loads[1].wait()
    loads[2].wait()
    lax.fori_loop(0, BLK_DEV // 2, fill, 0)
    send(slope, CAP)
    pltpu.make_async_copy(out, out, sem).wait()


def pack(targets, points, hidden, upstream, devices):
    anywhere = pl.BlockSpec(memory_space=pl.ANY)
    return pl.pallas_call(
        pack_kernel,
        in_specs=[pl.BlockSpec(memory_space=pltpu.SMEM), anywhere, anywhere, anywhere],
        out_specs=[anywhere, pl.BlockSpec(memory_space=pltpu.VMEM)],
        out_shape=[
            jax.ShapeDtypeStruct((devices, 2 * CAP, BS, C), jnp.bfloat16),
            jax.ShapeDtypeStruct((BLK_DEV, BS, C), jnp.bfloat16),
        ],
        scratch_shapes=[pltpu.VMEM((BLK_DEV, BS, C), jnp.bfloat16)] * 3
        + [pltpu.SemaphoreType.DMA(()), pltpu.SemaphoreType.DMA((3,))],
        compiler_params=pltpu.CompilerParams(vmem_limit_bytes=VMEM),
        cost_estimate=pl.CostEstimate(flops=10 * MIB, bytes_accessed=12 * MIB, transcendentals=0),
        name="pack",
    )(targets, points, hidden, upstream)


def pixel_kernel(
    neighbors, hidden, upstream, mixing, weight, slope, mixed, sums, first, last, total
):
    q = pl.program_id(0)

    @pl.when(q == 0)
    def _():
        total[...] = jnp.zeros_like(total)

    values = slope_of(upstream[...], hidden[...])
    slope[...] = values
    wide = values.astype(jnp.float32)
    for r in range(2):
        first[pl.ds(2 * q + r, 1), :] = wide[r, 0:1, :]
        last[pl.ds(2 * q + r, 1), :] = wide[r, COLS_DEV - 1 : COLS_DEV, :]
    projected = lax.dot_general(
        values.reshape(PIXB, C),
        weight[...],
        (((1,), (1,)), ((), ())),
        preferred_element_type=jnp.float32,
    ).astype(jnp.bfloat16)
    mixed[0] = projected
    term = lax.dot_general(
        mixing[0], projected, (((0,), (0,)), ((), ())), preferred_element_type=jnp.float32
    )
    for k in range(K):
        slot = neighbors[k, q]
        total[slot] += term[k * BS : (k + 1) * BS]

    @pl.when(q == PB - 1)
    def _():
        def body(i, carry):
            sums[i] = total[i].astype(jnp.bfloat16)
            return carry

        lax.fori_loop(0, total.shape[0], body, 0)


def pixel_part(neighbors, hidden, upstream, mixing, weight, slots):
    rows = pl.BlockSpec((2, COLS_DEV, C), lambda q, n: (q, 0, 0))
    return pl.pallas_call(
        pixel_kernel,
        grid_spec=pltpu.PrefetchScalarGridSpec(
            num_scalar_prefetch=1,
            grid=(PB,),
            in_specs=[
                rows,
                rows,
                pl.BlockSpec((1, PIXB, K * BS), lambda q, n: (q, 0, 0)),
                pl.BlockSpec((C, C), lambda q, n: (0, 0)),
            ],
            out_specs=[
                rows,
                pl.BlockSpec((1, PIXB, C), lambda q, n: (q, 0, 0)),
                pl.BlockSpec((slots, BS, C), lambda q, n: (0, 0, 0)),
                pl.BlockSpec((ROWS_DEV, C), lambda q, n: (0, 0)),
                pl.BlockSpec((ROWS_DEV, C), lambda q, n: (0, 0)),
            ],
            scratch_shapes=[pltpu.VMEM((slots, BS, C), jnp.float32)],
        ),
        out_shape=[
            jax.ShapeDtypeStruct((ROWS_DEV, COLS_DEV, C), jnp.bfloat16),
            jax.ShapeDtypeStruct((PB, PIXB, C), jnp.bfloat16),
            jax.ShapeDtypeStruct((slots, BS, C), jnp.bfloat16),
            jax.ShapeDtypeStruct((ROWS_DEV, C), jnp.float32),
            jax.ShapeDtypeStruct((ROWS_DEV, C), jnp.float32),
        ],
        compiler_params=pltpu.CompilerParams(vmem_limit_bytes=VMEM),
        cost_estimate=pl.CostEstimate(
            flops=1200 * MIB, bytes_accessed=18 * MIB, transcendentals=MIB
        ),
        name="pixel_part",
    )(neighbors, hidden, upstream, mixing, weight)


def main_kernel(
    neighbors, incoming, mixed, pixels, mixing, upstream, slope, above, below, left, right, kernel,
    mixing_gradient, pixel_gradient, totals, left_side, right_side,
):
    q = pl.program_id(0)
    for k in range(K):
        slot = neighbors[k, q]
        owner = lax.div(slot, CAP)
        place = lax.rem(slot, CAP)
        right_side[k * BS : (k + 1) * BS, 0:C] = incoming[owner, place]
        right_side[k * BS : (k + 1) * BS, C : 2 * C] = incoming[owner, CAP + place]
    left_side[:, 0:C] = mixed[0]
    left_side[:, C : 2 * C] = pixels[...].reshape(PIXB, C)
    mixing_gradient[0] = lax.dot_general(
        left_side[...],
        right_side[...],
        (((1,), (1,)), ((), ())),
        preferred_element_type=jnp.float32,
    ).astype(jnp.bfloat16)
    term = jnp.dot(mixing[0], right_side[:, C : 2 * C], preferred_element_type=jnp.float32)
    column = lax.broadcasted_iota(jnp.int32, (COLS_DEV, C), 0)
    before = jnp.maximum(2 * q - 1, 0)
    after = jnp.minimum(2 * q + 2, ROWS_DEV - 1)
    top = q == 0
    bottom = q == PB - 1

    def wide(piece):
        return piece.astype(jnp.float32)

    rows = [
        jnp.where(top, wide(above[0]), wide(slope[before])),
        wide(slope[2 * q]),
        wide(slope[2 * q + 1]),
        jnp.where(bottom, wide(below[0]), wide(slope[after])),
    ]

    def rim(side):
        zero = jnp.zeros((1, C), jnp.float32)
        return [
            jnp.where(top, zero, side[pl.ds(before, 1), :]),
            side[pl.ds(2 * q, 1), :],
            side[pl.ds(2 * q + 1, 1), :],
            jnp.where(bottom, zero, side[pl.ds(after, 1), :]),
        ]

    rims = {0: rim(right), 2: rim(left)}
    gains = [[kernel[a, e : e + 1, :] for e in range(3)] for a in range(3)]

    def mix(pieces, r, e):
        return sum(gains[a][e] * pieces[r + 2 - a] for a in range(3))

    for r in range(2):
        total = wide(upstream[r]) + term[r * COLS_DEV : (r + 1) * COLS_DEV]
        total = total + mix(rows, r, 1)
        ahead = pltpu.roll(mix(rows, r, 0), COLS_DEV - 1, 0)
        total = total + jnp.where(column == COLS_DEV - 1, mix(rims[0], r, 0), ahead)
        behind = pltpu.roll(mix(rows, r, 2), 1, 0)
        total = total + jnp.where(column == 0, mix(rims[2], r, 2), behind)
        pixel_gradient[r] = total.astype(jnp.bfloat16)

        @pl.when(q == r * (PB - 1))
        def _():
            totals[2 * r : 2 * r + 1] = total[0:1]
            totals[2 * r + 1 : 2 * r + 2] = total[COLS_DEV - 1 : COLS_DEV]


def main_part(
    neighbors, incoming, mixed, pixels, mixing, upstream, slope, above, below, left, right, kernel
):
    rows = pl.BlockSpec((2, COLS_DEV, C), lambda q, n: (q, 0, 0))
    once = pl.Buffered(1)
    return pl.pallas_call(
        main_kernel,
        grid_spec=pltpu.PrefetchScalarGridSpec(
            num_scalar_prefetch=1,
            grid=(PB,),
            in_specs=[
                pl.BlockSpec(incoming.shape, lambda q, n: (0, 0, 0, 0), pipeline_mode=once),
                pl.BlockSpec((1, PIXB, C), lambda q, n: (q, 0, 0)),
                rows,
                pl.BlockSpec((1, PIXB, K * BS), lambda q, n: (q, 0, 0)),
                rows,
                pl.BlockSpec(slope.shape, lambda q, n: (0, 0, 0), pipeline_mode=once),
                pl.BlockSpec(above.shape, lambda q, n: (0, 0, 0)),
                pl.BlockSpec(below.shape, lambda q, n: (0, 0, 0)),
                pl.BlockSpec(left.shape, lambda q, n: (0, 0)),
                pl.BlockSpec(right.shape, lambda q, n: (0, 0)),
                pl.BlockSpec((3, 3, C), lambda q, n: (0, 0, 0)),
            ],
            out_specs=[
                pl.BlockSpec((1, PIXB, K * BS), lambda q, n: (q, 0, 0)),
                rows,
                pl.BlockSpec((4, C), lambda q, n: (0, 0)),
            ],
            scratch_shapes=[
                pltpu.VMEM((PIXB, 2 * C), jnp.bfloat16),
                pltpu.VMEM((K * BS, 2 * C), jnp.bfloat16),
            ],
        ),
        out_shape=[
            jax.ShapeDtypeStruct((PB, PIXB, K * BS), jnp.bfloat16),
            jax.ShapeDtypeStruct((ROWS_DEV, COLS_DEV, C), jnp.bfloat16),
            jax.ShapeDtypeStruct((4, C), jnp.float32),
        ],
        compiler_params=pltpu.CompilerParams(vmem_limit_bytes=VMEM),
        cost_estimate=pl.CostEstimate(
            flops=2600 * MIB, bytes_accessed=30 * MIB, transcendentals=0
        ),
        name="main_part",
    )(
        neighbors, incoming, mixed, pixels, mixing, upstream, slope, above, below, left, right,
        kernel,
    )


def return_kernel(
    targets, received, base, totals, gains, corner_0, corner_1, corner_2, corner_3, gradient,
    out, fixed, landed, sems, tiles, tile_sems, *sums,
):
    parts = received.shape[0] // OWNERS

    def fetch(i):
        part = pl.ds(i * OWNERS, OWNERS)
        return pltpu.make_async_copy(received.at[part], landed.at[part], sems.at[i])

    def place(ref, i):
        return ref.at[i // 2 * (ROWS_DEV - 1), pl.ds(i % 2 * (COLS_DEV - 16), 16)]

    def load(i):
        return pltpu.make_async_copy(place(gradient, i), tiles.at[i], tile_sems.at[i])

    def store(i):
        return pltpu.make_async_copy(tiles.at[i], place(fixed, i), tile_sems.at[i])

    for i in range(4):
        load(i).start()
    for i in range(parts):
        fetch(i).start()
    sums[0][...] = base[...]
    for total in sums[1:]:
        total[...] = jnp.zeros_like(total)
    row = lax.broadcasted_iota(jnp.int32, (16, C), 0)
    for i, corner in enumerate((corner_0, corner_1, corner_2, corner_3)):
        load(i).wait()
        value = totals[i : i + 1, :] + gains[i : i + 1, :] * corner[...]
        tile = jnp.where(row == i % 2 * 15, value, tiles[i].astype(jnp.float32))
        tiles[i] = tile.astype(jnp.bfloat16)
        store(i).start()

    def body(i, carry):
        fetch(i).wait()
        for j in range(OWNERS):
            for s in range(CAP):
                o = i * OWNERS + j
                block = targets[0, s, o]
                sums[(j * CAP + s) % SPREAD][block] += landed[o, s].astype(jnp.float32)
        return carry

    lax.fori_loop(0, parts, body, 0)
    whole = sums[0][...]
    for total in sums[1:]:
        whole = whole + total[...]
    out[...] = whole.astype(jnp.bfloat16)
    for i in range(4):
        store(i).wait()


def return_part(targets, received, base, totals, gains, corners, gradient):
    whole = pl.BlockSpec(memory_space=pltpu.VMEM)
    anywhere = pl.BlockSpec(memory_space=pl.ANY)
    parts = received.shape[0] // OWNERS
    return pl.pallas_call(
        return_kernel,
        in_specs=[pl.BlockSpec(memory_space=pltpu.SMEM), anywhere]
        + [whole] * 7
        + [anywhere],
        out_specs=[whole, anywhere],
        scratch_shapes=[
            pltpu.VMEM(received.shape, jnp.bfloat16),
            pltpu.SemaphoreType.DMA((parts,)),
            pltpu.VMEM((4, 16, C), jnp.bfloat16),
            pltpu.SemaphoreType.DMA((4,)),
        ]
        + [pltpu.VMEM((BLK_DEV, BS, C), jnp.float32)] * SPREAD,
        out_shape=[
            jax.ShapeDtypeStruct((BLK_DEV, BS, C), jnp.bfloat16),
            jax.ShapeDtypeStruct(gradient.shape, jnp.bfloat16),
        ],
        input_output_aliases={9: 1},
        compiler_params=pltpu.CompilerParams(vmem_limit_bytes=VMEM),
        cost_estimate=pl.CostEstimate(flops=4 * MIB, bytes_accessed=6 * MIB, transcendentals=0),
        name="return_part",
    )(targets, received, base, totals, gains, *corners, gradient)


def shifted(block, tiles, cams, tile_step, cam_step):
    pairs = []
    for t in range(tiles):
        for c in range(cams):
            strip = (t + 1) % STRIPS + tile_step
            cam = c + cam_step
            if 0 <= strip < STRIPS and 0 <= cam < cams:
                pairs.append((t * cams + c, (t + tile_step) % tiles * cams + cam))
    return lax.ppermute(block, ("tile", "cam"), pairs)


def per_device(
    pixels,
    pixel_hidden,
    pixel_upstream,
    points,
    point_hidden,
    point_upstream,
    mixing,
    neighbors,
    send_list,
    pixel_weight,
    point_weight,
    kernel,
):
    tiles = lax.axis_size("tile")
    cams = lax.axis_size("cam")
    devices = tiles * cams
    slots = devices * CAP
    targets = jnp.transpose(send_list, (0, 2, 1))
    reads = neighbors.T
    blocks = (BLK_DEV, BS, C)
    outgoing, point_slope = pack(
        targets,
        points.reshape(blocks),
        point_hidden.reshape(blocks),
        point_upstream.reshape(blocks),
        devices,
    )
    outgoing, reads = lax.optimization_barrier((outgoing, reads))
    incoming = lax.all_to_all(
        outgoing, ("tile", "cam"), split_axis=0, concat_axis=0, tiled=True
    )
    pixel_slope, mixed, sums, first, last = pixel_part(
        reads, pixel_hidden, pixel_upstream, mixing, pixel_weight, slots
    )
    move = functools.partial(shifted, tiles=tiles, cams=cams)
    above = move(pixel_slope[-1:], tile_step=0, cam_step=1)
    below = move(pixel_slope[:1], tile_step=0, cam_step=-1)
    rim_left = move(last, tile_step=1, cam_step=0)
    rim_right = move(first, tile_step=-1, cam_step=0)
    sums, incoming, above, below, rim_left, rim_right, point_slope = lax.optimization_barrier(
        (sums, incoming, above, below, rim_left, rim_right, point_slope)
    )
    received = lax.all_to_all(
        sums.reshape(devices, CAP, BS, C),
        ("tile", "cam"),
        split_axis=0,
        concat_axis=0,
        tiled=True,
    )
    base = point_upstream.astype(jnp.float32) + jnp.dot(
        point_slope.reshape(BLK_DEV * BS, C), point_weight.T, preferred_element_type=jnp.float32
    )
    base, first, last = lax.optimization_barrier((base, first, last))
    corners = (
        move(last[-1:], tile_step=1, cam_step=1),
        move(first[-1:], tile_step=-1, cam_step=1),
        move(last[:1], tile_step=1, cam_step=-1),
        move(first[:1], tile_step=-1, cam_step=-1),
    )
    mixing_gradient, pixel_gradient, totals = main_part(
        reads, incoming, mixed, pixels, mixing, pixel_upstream,
        pixel_slope, above, below, rim_left, rim_right, kernel,
    )
    gains = jnp.stack([kernel[2, 2], kernel[2, 0], kernel[0, 2], kernel[0, 0]])
    point_gradient, pixel_gradient = return_part(
        targets, received, base.reshape(blocks), totals, gains, corners, pixel_gradient
    )
    return (pixel_gradient, point_gradient.reshape(BLK_DEV * BS, C), mixing_gradient)


def solution(mesh):
    return jax.shard_map(
        per_device,
        mesh=mesh,
        in_specs=(
            P("cam", "tile", None),
            P("cam", "tile", None),
            P("cam", "tile", None),
            P(("tile", "cam"), None),
            P(("tile", "cam"), None),
            P(("tile", "cam"), None),
            P(("tile", "cam"), None, None),
            P(("tile", "cam"), None),
            P(("tile", "cam"), None, None),
            P(),
            P(),
            P(),
        ),
        out_specs=(
            P("cam", "tile", None),
            P(("tile", "cam"), None),
            P(("tile", "cam"), None, None),
        ),
        check_vma=False,
    )
```

```python
import functools

import jax
import jax.numpy as jnp
from jax import lax
from jax.experimental import pallas as pl
from jax.experimental.pallas import tpu as pltpu
from jax.sharding import PartitionSpec as P

C = 128
ROWS_DEV = 64
COLS_DEV = 128
K = 6
BS = 64
CAP = 2
BLK_DEV = 32
PB = 32
PIXB = 256
STRIPS = 4
MIB = 1024 * 1024
VMEM = 60 * MIB
DESTS = 4
OWNERS = 16
SPREAD = 2


def slope_of(upstream, hidden):
    argument = hidden.astype(jnp.float32)
    logistic = 0.5 + 0.5 * jnp.tanh(0.5 * argument)
    slope = logistic * (1.0 + argument * (1.0 - logistic))
    return (upstream.astype(jnp.float32) * slope).astype(jnp.bfloat16)


def pack_kernel(targets, points, hidden, upstream, out, slope, sem):
    def send(source, first):
        def body(i, carry):
            for j in range(DESTS):
                d = i * DESTS + j
                for s in range(CAP):
                    block = source.at[targets[0, s, d]]
                    pltpu.make_async_copy(block, out.at[d, first + s], sem).start()
            return carry

        lax.fori_loop(0, out.shape[0] // DESTS, body, 0)

    def fill(i, carry):
        part = pl.ds(2 * i, 2)
        slope[part] = slope_of(upstream[part], hidden[part])
        return carry

    send(points, 0)
    lax.fori_loop(0, BLK_DEV // 2, fill, 0)
    send(slope, CAP)
    pltpu.make_async_copy(out, out, sem).wait()


def pack(targets, points, hidden, upstream, devices):
    whole = pl.BlockSpec(memory_space=pltpu.VMEM)
    return pl.pallas_call(
        pack_kernel,
        in_specs=[pl.BlockSpec(memory_space=pltpu.SMEM), whole, whole, whole],
        out_specs=[pl.BlockSpec(memory_space=pl.ANY), whole],
        out_shape=[
            jax.ShapeDtypeStruct((devices, 2 * CAP, BS, C), jnp.bfloat16),
            jax.ShapeDtypeStruct((BLK_DEV, BS, C), jnp.bfloat16),
        ],
        scratch_shapes=[pltpu.SemaphoreType.DMA(())],
        compiler_params=pltpu.CompilerParams(vmem_limit_bytes=VMEM),
        cost_estimate=pl.CostEstimate(flops=10 * MIB, bytes_accessed=12 * MIB, transcendentals=0),
        name="pack",
    )(targets, points, hidden, upstream)


def pixel_kernel(
    neighbors, hidden, upstream, mixing, weight, slope, mixed, sums, first, last, total
):
    q = pl.program_id(0)

    @pl.when(q == 0)
    def _():
        total[...] = jnp.zeros_like(total)

    values = slope_of(upstream[...], hidden[...])
    slope[...] = values
    wide = values.astype(jnp.float32)
    for r in range(2):
        first[pl.ds(2 * q + r, 1), :] = wide[r, 0:1, :]
        last[pl.ds(2 * q + r, 1), :] = wide[r, COLS_DEV - 1 : COLS_DEV, :]
    projected = lax.dot_general(
        values.reshape(PIXB, C),
        weight[...],
        (((1,), (1,)), ((), ())),
        preferred_element_type=jnp.float32,
    ).astype(jnp.bfloat16)
    mixed[0] = projected
    term = lax.dot_general(
        mixing[0], projected, (((0,), (0,)), ((), ())), preferred_element_type=jnp.float32
    )
    for k in range(K):
        slot = neighbors[k, q]
        total[slot] += term[k * BS : (k + 1) * BS]

    @pl.when(q == PB - 1)
    def _():
        def body(i, carry):
            sums[i] = total[i].astype(jnp.bfloat16)
            return carry

        lax.fori_loop(0, total.shape[0], body, 0)


def pixel_part(neighbors, hidden, upstream, mixing, weight, slots):
    rows = pl.BlockSpec((2, COLS_DEV, C), lambda q, n: (q, 0, 0))
    return pl.pallas_call(
        pixel_kernel,
        grid_spec=pltpu.PrefetchScalarGridSpec(
            num_scalar_prefetch=1,
            grid=(PB,),
            in_specs=[
                rows,
                rows,
                pl.BlockSpec((1, PIXB, K * BS), lambda q, n: (q, 0, 0)),
                pl.BlockSpec((C, C), lambda q, n: (0, 0)),
            ],
            out_specs=[
                rows,
                pl.BlockSpec((1, PIXB, C), lambda q, n: (q, 0, 0)),
                pl.BlockSpec((slots, BS, C), lambda q, n: (0, 0, 0)),
                pl.BlockSpec((ROWS_DEV, C), lambda q, n: (0, 0)),
                pl.BlockSpec((ROWS_DEV, C), lambda q, n: (0, 0)),
            ],
            scratch_shapes=[pltpu.VMEM((slots, BS, C), jnp.float32)],
        ),
        out_shape=[
            jax.ShapeDtypeStruct((ROWS_DEV, COLS_DEV, C), jnp.bfloat16),
            jax.ShapeDtypeStruct((PB, PIXB, C), jnp.bfloat16),
            jax.ShapeDtypeStruct((slots, BS, C), jnp.bfloat16),
            jax.ShapeDtypeStruct((ROWS_DEV, C), jnp.float32),
            jax.ShapeDtypeStruct((ROWS_DEV, C), jnp.float32),
        ],
        compiler_params=pltpu.CompilerParams(vmem_limit_bytes=VMEM),
        cost_estimate=pl.CostEstimate(
            flops=1200 * MIB, bytes_accessed=18 * MIB, transcendentals=MIB
        ),
        name="pixel_part",
    )(neighbors, hidden, upstream, mixing, weight)


def main_kernel(
    neighbors, incoming, mixed, pixels, mixing, upstream, slope, above, below, left, right, kernel,
    mixing_gradient, pixel_gradient, totals, left_side, right_side,
):
    q = pl.program_id(0)
    for k in range(K):
        slot = neighbors[k, q]
        owner = lax.div(slot, CAP)
        place = lax.rem(slot, CAP)
        right_side[k * BS : (k + 1) * BS, 0:C] = incoming[owner, place]
        right_side[k * BS : (k + 1) * BS, C : 2 * C] = incoming[owner, CAP + place]
    left_side[:, 0:C] = mixed[0]
    left_side[:, C : 2 * C] = pixels[...].reshape(PIXB, C)
    mixing_gradient[0] = lax.dot_general(
        left_side[...],
        right_side[...],
        (((1,), (1,)), ((), ())),
        preferred_element_type=jnp.float32,
    ).astype(jnp.bfloat16)
    term = jnp.dot(mixing[0], right_side[:, C : 2 * C], preferred_element_type=jnp.float32)
    column = lax.broadcasted_iota(jnp.int32, (COLS_DEV, C), 0)
    before = jnp.maximum(2 * q - 1, 0)
    after = jnp.minimum(2 * q + 2, ROWS_DEV - 1)
    top = q == 0
    bottom = q == PB - 1

    def wide(piece):
        return piece.astype(jnp.float32)

    rows = [
        jnp.where(top, wide(above[0]), wide(slope[before])),
        wide(slope[2 * q]),
        wide(slope[2 * q + 1]),
        jnp.where(bottom, wide(below[0]), wide(slope[after])),
    ]

    def rim(side):
        zero = jnp.zeros((1, C), jnp.float32)
        return [
            jnp.where(top, zero, side[pl.ds(before, 1), :]),
            side[pl.ds(2 * q, 1), :],
            side[pl.ds(2 * q + 1, 1), :],
            jnp.where(bottom, zero, side[pl.ds(after, 1), :]),
        ]

    rims = {0: rim(right), 2: rim(left)}
    gains = [[kernel[a, e : e + 1, :] for e in range(3)] for a in range(3)]

    def mix(pieces, r, e):
        return sum(gains[a][e] * pieces[r + 2 - a] for a in range(3))

    for r in range(2):
        total = wide(upstream[r]) + term[r * COLS_DEV : (r + 1) * COLS_DEV]
        total = total + mix(rows, r, 1)
        ahead = pltpu.roll(mix(rows, r, 0), COLS_DEV - 1, 0)
        total = total + jnp.where(column == COLS_DEV - 1, mix(rims[0], r, 0), ahead)
        behind = pltpu.roll(mix(rows, r, 2), 1, 0)
        total = total + jnp.where(column == 0, mix(rims[2], r, 2), behind)
        pixel_gradient[r] = total.astype(jnp.bfloat16)

        @pl.when(q == r * (PB - 1))
        def _():
            totals[2 * r : 2 * r + 1] = total[0:1]
            totals[2 * r + 1 : 2 * r + 2] = total[COLS_DEV - 1 : COLS_DEV]


def main_part(
    neighbors, incoming, mixed, pixels, mixing, upstream, slope, above, below, left, right, kernel
):
    rows = pl.BlockSpec((2, COLS_DEV, C), lambda q, n: (q, 0, 0))
    once = pl.Buffered(1)
    return pl.pallas_call(
        main_kernel,
        grid_spec=pltpu.PrefetchScalarGridSpec(
            num_scalar_prefetch=1,
            grid=(PB,),
            in_specs=[
                pl.BlockSpec(incoming.shape, lambda q, n: (0, 0, 0, 0), pipeline_mode=once),
                pl.BlockSpec((1, PIXB, C), lambda q, n: (q, 0, 0)),
                rows,
                pl.BlockSpec((1, PIXB, K * BS), lambda q, n: (q, 0, 0)),
                rows,
                pl.BlockSpec(slope.shape, lambda q, n: (0, 0, 0), pipeline_mode=once),
                pl.BlockSpec(above.shape, lambda q, n: (0, 0, 0)),
                pl.BlockSpec(below.shape, lambda q, n: (0, 0, 0)),
                pl.BlockSpec(left.shape, lambda q, n: (0, 0)),
                pl.BlockSpec(right.shape, lambda q, n: (0, 0)),
                pl.BlockSpec((3, 3, C), lambda q, n: (0, 0, 0)),
            ],
            out_specs=[
                pl.BlockSpec((1, PIXB, K * BS), lambda q, n: (q, 0, 0)),
                rows,
                pl.BlockSpec((4, C), lambda q, n: (0, 0)),
            ],
            scratch_shapes=[
                pltpu.VMEM((PIXB, 2 * C), jnp.bfloat16),
                pltpu.VMEM((K * BS, 2 * C), jnp.bfloat16),
            ],
        ),
        out_shape=[
            jax.ShapeDtypeStruct((PB, PIXB, K * BS), jnp.bfloat16),
            jax.ShapeDtypeStruct((ROWS_DEV, COLS_DEV, C), jnp.bfloat16),
            jax.ShapeDtypeStruct((4, C), jnp.float32),
        ],
        compiler_params=pltpu.CompilerParams(vmem_limit_bytes=VMEM),
        cost_estimate=pl.CostEstimate(
            flops=2600 * MIB, bytes_accessed=30 * MIB, transcendentals=0
        ),
        name="main_part",
    )(
        neighbors, incoming, mixed, pixels, mixing, upstream, slope, above, below, left, right,
        kernel,
    )


def return_kernel(
    targets, received, base, totals, gains, corner_0, corner_1, corner_2, corner_3, gradient,
    out, fixed, landed, sems, tiles, tile_sems, start, start_sem, *sums,
):
    parts = received.shape[0] // OWNERS

    def fetch(i):
        part = pl.ds(i * OWNERS, OWNERS)
        return pltpu.make_async_copy(received.at[part], landed.at[part], sems.at[i])

    def place(ref, i):
        return ref.at[i // 2 * (ROWS_DEV - 1), pl.ds(i % 2 * (COLS_DEV - 16), 16)]

    def load(i):
        return pltpu.make_async_copy(place(gradient, i), tiles.at[i], tile_sems.at[i])

    def store(i):
        return pltpu.make_async_copy(tiles.at[i], place(fixed, i), tile_sems.at[i])

    for i in range(4):
        load(i).start()
    for i in range(parts):
        fetch(i).start()
    first = pltpu.make_async_copy(base, start, start_sem)
    first.start()
    for total in sums:
        total[...] = jnp.zeros_like(total)
    row = lax.broadcasted_iota(jnp.int32, (16, C), 0)
    for i, corner in enumerate((corner_0, corner_1, corner_2, corner_3)):
        load(i).wait()
        value = totals[i : i + 1, :] + gains[i : i + 1, :] * corner[...]
        tile = jnp.where(row == i % 2 * 15, value, tiles[i].astype(jnp.float32))
        tiles[i] = tile.astype(jnp.bfloat16)
        store(i).start()

    def body(i, carry):
        fetch(i).wait()
        for j in range(OWNERS):
            for s in range(CAP):
                o = i * OWNERS + j
                block = targets[0, s, o]
                sums[(j * CAP + s) % SPREAD][block] += landed[o, s].astype(jnp.float32)
        return carry

    lax.fori_loop(0, parts, body, 0)
    first.wait()
    whole = start[...]
    for total in sums:
        whole = whole + total[...]
    out[...] = whole.astype(jnp.bfloat16)
    for i in range(4):
        store(i).wait()


def return_part(targets, received, base, totals, gains, corners, gradient):
    whole = pl.BlockSpec(memory_space=pltpu.VMEM)
    anywhere = pl.BlockSpec(memory_space=pl.ANY)
    parts = received.shape[0] // OWNERS
    return pl.pallas_call(
        return_kernel,
        in_specs=[pl.BlockSpec(memory_space=pltpu.SMEM), anywhere, anywhere]
        + [whole] * 6
        + [anywhere],
        out_specs=[whole, anywhere],
        scratch_shapes=[
            pltpu.VMEM(received.shape, jnp.bfloat16),
            pltpu.SemaphoreType.DMA((parts,)),
            pltpu.VMEM((4, 16, C), jnp.bfloat16),
            pltpu.SemaphoreType.DMA((4,)),
            pltpu.VMEM((BLK_DEV, BS, C), jnp.float32),
            pltpu.SemaphoreType.DMA(()),
        ]
        + [pltpu.VMEM((BLK_DEV, BS, C), jnp.float32)] * SPREAD,
        out_shape=[
            jax.ShapeDtypeStruct((BLK_DEV, BS, C), jnp.bfloat16),
            jax.ShapeDtypeStruct(gradient.shape, jnp.bfloat16),
        ],
        input_output_aliases={9: 1},
        compiler_params=pltpu.CompilerParams(vmem_limit_bytes=VMEM),
        cost_estimate=pl.CostEstimate(flops=4 * MIB, bytes_accessed=6 * MIB, transcendentals=0),
        name="return_part",
    )(targets, received, base, totals, gains, *corners, gradient)


def shifted(block, tiles, cams, tile_step, cam_step):
    pairs = []
    for t in range(tiles):
        for c in range(cams):
            strip = (t + 1) % STRIPS + tile_step
            cam = c + cam_step
            if 0 <= strip < STRIPS and 0 <= cam < cams:
                pairs.append((t * cams + c, (t + tile_step) % tiles * cams + cam))
    return lax.ppermute(block, ("tile", "cam"), pairs)


def per_device(
    pixels,
    pixel_hidden,
    pixel_upstream,
    points,
    point_hidden,
    point_upstream,
    mixing,
    neighbors,
    send_list,
    pixel_weight,
    point_weight,
    kernel,
):
    tiles = lax.axis_size("tile")
    cams = lax.axis_size("cam")
    devices = tiles * cams
    slots = devices * CAP
    targets = jnp.transpose(send_list, (0, 2, 1))
    reads = neighbors.T
    blocks = (BLK_DEV, BS, C)
    outgoing, point_slope = pack(
        targets,
        points.reshape(blocks),
        point_hidden.reshape(blocks),
        point_upstream.reshape(blocks),
        devices,
    )
    outgoing, reads = lax.optimization_barrier((outgoing, reads))
    incoming = lax.all_to_all(
        outgoing, ("tile", "cam"), split_axis=0, concat_axis=0, tiled=True
    )
    pixel_slope, mixed, sums, first, last = pixel_part(
        reads, pixel_hidden, pixel_upstream, mixing, pixel_weight, slots
    )
    move = functools.partial(shifted, tiles=tiles, cams=cams)
    above = move(pixel_slope[-1:], tile_step=0, cam_step=1)
    below = move(pixel_slope[:1], tile_step=0, cam_step=-1)
    rim_left = move(last, tile_step=1, cam_step=0)
    rim_right = move(first, tile_step=-1, cam_step=0)
    sums, incoming, above, below, rim_left, rim_right, point_slope = lax.optimization_barrier(
        (sums, incoming, above, below, rim_left, rim_right, point_slope)
    )
    received = lax.all_to_all(
        sums.reshape(devices, CAP, BS, C),
        ("tile", "cam"),
        split_axis=0,
        concat_axis=0,
        tiled=True,
    )
    base = point_upstream.astype(jnp.float32) + jnp.dot(
        point_slope.reshape(BLK_DEV * BS, C), point_weight.T, preferred_element_type=jnp.float32
    )
    base, first, last = lax.optimization_barrier((base, first, last))
    corners = (
        move(last[-1:], tile_step=1, cam_step=1),
        move(first[-1:], tile_step=-1, cam_step=1),
        move(last[:1], tile_step=1, cam_step=-1),
        move(first[:1], tile_step=-1, cam_step=-1),
    )
    mixing_gradient, pixel_gradient, totals = main_part(
        reads, incoming, mixed, pixels, mixing, pixel_upstream,
        pixel_slope, above, below, rim_left, rim_right, kernel,
    )
    gains = jnp.stack([kernel[2, 2], kernel[2, 0], kernel[0, 2], kernel[0, 0]])
    point_gradient, pixel_gradient = return_part(
        targets, received, base.reshape(blocks), totals, gains, corners, pixel_gradient
    )
    return (pixel_gradient, point_gradient.reshape(BLK_DEV * BS, C), mixing_gradient)


def solution(mesh):
    return jax.shard_map(
        per_device,
        mesh=mesh,
        in_specs=(
            P("cam", "tile", None),
            P("cam", "tile", None),
            P("cam", "tile", None),
            P(("tile", "cam"), None),
            P(("tile", "cam"), None),
            P(("tile", "cam"), None),
            P(("tile", "cam"), None, None),
            P(("tile", "cam"), None),
            P(("tile", "cam"), None, None),
            P(),
            P(),
            P(),
        ),
        out_specs=(
            P("cam", "tile", None),
            P(("tile", "cam"), None),
            P(("tile", "cam"), None, None),
        ),
        check_vma=False,
    )
```

```python
import functools

import jax
import jax.numpy as jnp
from jax import lax
from jax.experimental import pallas as pl
from jax.experimental.pallas import tpu as pltpu
from jax.sharding import PartitionSpec as P

C = 128
ROWS_DEV = 64
COLS_DEV = 128
K = 6
BS = 64
CAP = 2
BLK_DEV = 32
PB = 32
PIXB = 256
STRIPS = 4
MIB = 1024 * 1024
VMEM = 60 * MIB
DESTS = 4
OWNERS = 16
SPREAD = 2


def peer_at(position):
    return (position & 99) | ((position >> 2) & 4) | ((position & 12) << 1)


def position_of(peer):
    return (peer & 99) | ((peer & 4) << 2) | ((peer >> 1) & 12)


def slope_of(upstream, hidden):
    argument = hidden.astype(jnp.float32)
    logistic = 0.5 + 0.5 * jnp.tanh(0.5 * argument)
    slope = logistic * (1.0 + argument * (1.0 - logistic))
    return (upstream.astype(jnp.float32) * slope).astype(jnp.bfloat16)


def pack_kernel(targets, points, hidden, upstream, out, slope, sem):
    def send(source, first):
        def body(i, carry):
            for j in range(DESTS):
                d = i * DESTS + j
                for s in range(CAP):
                    block = source.at[targets[0, s, peer_at(d)]]
                    pltpu.make_async_copy(block, out.at[d, first + s], sem).start()
            return carry

        lax.fori_loop(0, out.shape[0] // DESTS, body, 0)

    def fill(i, carry):
        part = pl.ds(2 * i, 2)
        slope[part] = slope_of(upstream[part], hidden[part])
        return carry

    send(points, 0)
    lax.fori_loop(0, BLK_DEV // 2, fill, 0)
    send(slope, CAP)
    pltpu.make_async_copy(out, out, sem).wait()


def pack(targets, points, hidden, upstream, devices):
    whole = pl.BlockSpec(memory_space=pltpu.VMEM)
    return pl.pallas_call(
        pack_kernel,
        in_specs=[pl.BlockSpec(memory_space=pltpu.SMEM), whole, whole, whole],
        out_specs=[pl.BlockSpec(memory_space=pl.ANY), whole],
        out_shape=[
            jax.ShapeDtypeStruct((devices, 2 * CAP, BS, C), jnp.bfloat16),
            jax.ShapeDtypeStruct((BLK_DEV, BS, C), jnp.bfloat16),
        ],
        scratch_shapes=[pltpu.SemaphoreType.DMA(())],
        compiler_params=pltpu.CompilerParams(vmem_limit_bytes=VMEM),
        cost_estimate=pl.CostEstimate(flops=10 * MIB, bytes_accessed=12 * MIB, transcendentals=0),
        name="pack",
    )(targets, points, hidden, upstream)


def pixel_kernel(
    neighbors, hidden, upstream, mixing, weight, slope, mixed, sums, first, last, total
):
    q = pl.program_id(0)

    @pl.when(q == 0)
    def _():
        total[...] = jnp.zeros_like(total)

    values = slope_of(upstream[...], hidden[...])
    slope[...] = values
    wide = values.astype(jnp.float32)
    for r in range(2):
        first[pl.ds(2 * q + r, 1), :] = wide[r, 0:1, :]
        last[pl.ds(2 * q + r, 1), :] = wide[r, COLS_DEV - 1 : COLS_DEV, :]
    projected = lax.dot_general(
        values.reshape(PIXB, C),
        weight[...],
        (((1,), (1,)), ((), ())),
        preferred_element_type=jnp.float32,
    ).astype(jnp.bfloat16)
    mixed[0] = projected
    term = lax.dot_general(
        mixing[0], projected, (((0,), (0,)), ((), ())), preferred_element_type=jnp.float32
    )
    for k in range(K):
        slot = position_of(lax.div(neighbors[k, q], CAP)) * CAP + lax.rem(neighbors[k, q], CAP)
        total[slot] += term[k * BS : (k + 1) * BS]

    @pl.when(q == PB - 1)
    def _():
        def body(i, carry):
            sums[i] = total[i].astype(jnp.bfloat16)
            return carry

        lax.fori_loop(0, total.shape[0], body, 0)


def pixel_part(neighbors, hidden, upstream, mixing, weight, slots):
    rows = pl.BlockSpec((2, COLS_DEV, C), lambda q, n: (q, 0, 0))
    return pl.pallas_call(
        pixel_kernel,
        grid_spec=pltpu.PrefetchScalarGridSpec(
            num_scalar_prefetch=1,
            grid=(PB,),
            in_specs=[
                rows,
                rows,
                pl.BlockSpec((1, PIXB, K * BS), lambda q, n: (q, 0, 0)),
                pl.BlockSpec((C, C), lambda q, n: (0, 0)),
            ],
            out_specs=[
                rows,
                pl.BlockSpec((1, PIXB, C), lambda q, n: (q, 0, 0)),
                pl.BlockSpec((slots, BS, C), lambda q, n: (0, 0, 0)),
                pl.BlockSpec((ROWS_DEV, C), lambda q, n: (0, 0)),
                pl.BlockSpec((ROWS_DEV, C), lambda q, n: (0, 0)),
            ],
            scratch_shapes=[pltpu.VMEM((slots, BS, C), jnp.float32)],
        ),
        out_shape=[
            jax.ShapeDtypeStruct((ROWS_DEV, COLS_DEV, C), jnp.bfloat16),
            jax.ShapeDtypeStruct((PB, PIXB, C), jnp.bfloat16),
            jax.ShapeDtypeStruct((slots, BS, C), jnp.bfloat16),
            jax.ShapeDtypeStruct((ROWS_DEV, C), jnp.float32),
            jax.ShapeDtypeStruct((ROWS_DEV, C), jnp.float32),
        ],
        compiler_params=pltpu.CompilerParams(vmem_limit_bytes=VMEM),
        cost_estimate=pl.CostEstimate(
            flops=1200 * MIB, bytes_accessed=18 * MIB, transcendentals=MIB
        ),
        name="pixel_part",
    )(neighbors, hidden, upstream, mixing, weight)


def main_kernel(
    neighbors, incoming, mixed, pixels, mixing, upstream, slope, above, below, left, right, kernel,
    mixing_gradient, pixel_gradient, totals, left_side, right_side,
):
    q = pl.program_id(0)
    for k in range(K):
        slot = neighbors[k, q]
        owner = position_of(lax.div(slot, CAP))
        place = lax.rem(slot, CAP)
        right_side[k * BS : (k + 1) * BS, 0:C] = incoming[owner, place]
        right_side[k * BS : (k + 1) * BS, C : 2 * C] = incoming[owner, CAP + place]
    left_side[:, 0:C] = mixed[0]
    left_side[:, C : 2 * C] = pixels[...].reshape(PIXB, C)
    mixing_gradient[0] = lax.dot_general(
        left_side[...],
        right_side[...],
        (((1,), (1,)), ((), ())),
        preferred_element_type=jnp.float32,
    ).astype(jnp.bfloat16)
    term = jnp.dot(mixing[0], right_side[:, C : 2 * C], preferred_element_type=jnp.float32)
    column = lax.broadcasted_iota(jnp.int32, (COLS_DEV, C), 0)
    before = jnp.maximum(2 * q - 1, 0)
    after = jnp.minimum(2 * q + 2, ROWS_DEV - 1)
    top = q == 0
    bottom = q == PB - 1

    def wide(piece):
        return piece.astype(jnp.float32)

    rows = [
        jnp.where(top, wide(above[0]), wide(slope[before])),
        wide(slope[2 * q]),
        wide(slope[2 * q + 1]),
        jnp.where(bottom, wide(below[0]), wide(slope[after])),
    ]

    def rim(side):
        zero = jnp.zeros((1, C), jnp.float32)
        return [
            jnp.where(top, zero, side[pl.ds(before, 1), :]),
            side[pl.ds(2 * q, 1), :],
            side[pl.ds(2 * q + 1, 1), :],
            jnp.where(bottom, zero, side[pl.ds(after, 1), :]),
        ]

    rims = {0: rim(right), 2: rim(left)}
    gains = [[kernel[a, e : e + 1, :] for e in range(3)] for a in range(3)]

    def mix(pieces, r, e):
        return sum(gains[a][e] * pieces[r + 2 - a] for a in range(3))

    for r in range(2):
        total = wide(upstream[r]) + term[r * COLS_DEV : (r + 1) * COLS_DEV]
        total = total + mix(rows, r, 1)
        ahead = pltpu.roll(mix(rows, r, 0), COLS_DEV - 1, 0)
        total = total + jnp.where(column == COLS_DEV - 1, mix(rims[0], r, 0), ahead)
        behind = pltpu.roll(mix(rows, r, 2), 1, 0)
        total = total + jnp.where(column == 0, mix(rims[2], r, 2), behind)
        pixel_gradient[r] = total.astype(jnp.bfloat16)

        @pl.when(q == r * (PB - 1))
        def _():
            totals[2 * r : 2 * r + 1] = total[0:1]
            totals[2 * r + 1 : 2 * r + 2] = total[COLS_DEV - 1 : COLS_DEV]


def main_part(
    neighbors, incoming, mixed, pixels, mixing, upstream, slope, above, below, left, right, kernel
):
    rows = pl.BlockSpec((2, COLS_DEV, C), lambda q, n: (q, 0, 0))
    once = pl.Buffered(1)
    return pl.pallas_call(
        main_kernel,
        grid_spec=pltpu.PrefetchScalarGridSpec(
            num_scalar_prefetch=1,
            grid=(PB,),
            in_specs=[
                pl.BlockSpec(incoming.shape, lambda q, n: (0, 0, 0, 0), pipeline_mode=once),
                pl.BlockSpec((1, PIXB, C), lambda q, n: (q, 0, 0)),
                rows,
                pl.BlockSpec((1, PIXB, K * BS), lambda q, n: (q, 0, 0)),
                rows,
                pl.BlockSpec(slope.shape, lambda q, n: (0, 0, 0), pipeline_mode=once),
                pl.BlockSpec(above.shape, lambda q, n: (0, 0, 0)),
                pl.BlockSpec(below.shape, lambda q, n: (0, 0, 0)),
                pl.BlockSpec(left.shape, lambda q, n: (0, 0)),
                pl.BlockSpec(right.shape, lambda q, n: (0, 0)),
                pl.BlockSpec((3, 3, C), lambda q, n: (0, 0, 0)),
            ],
            out_specs=[
                pl.BlockSpec((1, PIXB, K * BS), lambda q, n: (q, 0, 0)),
                rows,
                pl.BlockSpec((4, C), lambda q, n: (0, 0)),
            ],
            scratch_shapes=[
                pltpu.VMEM((PIXB, 2 * C), jnp.bfloat16),
                pltpu.VMEM((K * BS, 2 * C), jnp.bfloat16),
            ],
        ),
        out_shape=[
            jax.ShapeDtypeStruct((PB, PIXB, K * BS), jnp.bfloat16),
            jax.ShapeDtypeStruct((ROWS_DEV, COLS_DEV, C), jnp.bfloat16),
            jax.ShapeDtypeStruct((4, C), jnp.float32),
        ],
        compiler_params=pltpu.CompilerParams(vmem_limit_bytes=VMEM),
        cost_estimate=pl.CostEstimate(
            flops=2600 * MIB, bytes_accessed=30 * MIB, transcendentals=0
        ),
        name="main_part",
    )(
        neighbors, incoming, mixed, pixels, mixing, upstream, slope, above, below, left, right,
        kernel,
    )


def return_kernel(
    targets, received, base, totals, gains, corner_0, corner_1, corner_2, corner_3, gradient,
    out, fixed, landed, sems, tiles, tile_sems, start, start_sem, *sums,
):
    parts = received.shape[0] // OWNERS

    def fetch(i):
        part = pl.ds(i * OWNERS, OWNERS)
        return pltpu.make_async_copy(received.at[part], landed.at[part], sems.at[i])

    def place(ref, i):
        return ref.at[i // 2 * (ROWS_DEV - 1), pl.ds(i % 2 * (COLS_DEV - 16), 16)]

    def load(i):
        return pltpu.make_async_copy(place(gradient, i), tiles.at[i], tile_sems.at[i])

    def store(i):
        return pltpu.make_async_copy(tiles.at[i], place(fixed, i), tile_sems.at[i])

    for i in range(4):
        load(i).start()
    for i in range(parts):
        fetch(i).start()
    first = pltpu.make_async_copy(base, start, start_sem)
    first.start()
    for total in sums:
        total[...] = jnp.zeros_like(total)
    row = lax.broadcasted_iota(jnp.int32, (16, C), 0)
    for i, corner in enumerate((corner_0, corner_1, corner_2, corner_3)):
        load(i).wait()
        value = totals[i : i + 1, :] + gains[i : i + 1, :] * corner[...]
        tile = jnp.where(row == i % 2 * 15, value, tiles[i].astype(jnp.float32))
        tiles[i] = tile.astype(jnp.bfloat16)
        store(i).start()

    def body(i, carry):
        fetch(i).wait()
        for j in range(OWNERS):
            for s in range(CAP):
                o = i * OWNERS + j
                block = targets[0, s, peer_at(o)]
                sums[(j * CAP + s) % SPREAD][block] += landed[o, s].astype(jnp.float32)
        return carry

    lax.fori_loop(0, parts, body, 0)
    first.wait()
    whole = start[...]
    for total in sums:
        whole = whole + total[...]
    out[...] = whole.astype(jnp.bfloat16)
    for i in range(4):
        store(i).wait()


def return_part(targets, received, base, totals, gains, corners, gradient):
    whole = pl.BlockSpec(memory_space=pltpu.VMEM)
    anywhere = pl.BlockSpec(memory_space=pl.ANY)
    parts = received.shape[0] // OWNERS
    return pl.pallas_call(
        return_kernel,
        in_specs=[pl.BlockSpec(memory_space=pltpu.SMEM), anywhere, anywhere]
        + [whole] * 6
        + [anywhere],
        out_specs=[whole, anywhere],
        scratch_shapes=[
            pltpu.VMEM(received.shape, jnp.bfloat16),
            pltpu.SemaphoreType.DMA((parts,)),
            pltpu.VMEM((4, 16, C), jnp.bfloat16),
            pltpu.SemaphoreType.DMA((4,)),
            pltpu.VMEM((BLK_DEV, BS, C), jnp.float32),
            pltpu.SemaphoreType.DMA(()),
        ]
        + [pltpu.VMEM((BLK_DEV, BS, C), jnp.float32)] * SPREAD,
        out_shape=[
            jax.ShapeDtypeStruct((BLK_DEV, BS, C), jnp.bfloat16),
            jax.ShapeDtypeStruct(gradient.shape, jnp.bfloat16),
        ],
        input_output_aliases={9: 1},
        compiler_params=pltpu.CompilerParams(vmem_limit_bytes=VMEM),
        cost_estimate=pl.CostEstimate(flops=4 * MIB, bytes_accessed=6 * MIB, transcendentals=0),
        name="return_part",
    )(targets, received, base, totals, gains, *corners, gradient)


def shifted(block, tiles, cams, tile_step, cam_step):
    pairs = []
    for t in range(tiles):
        for c in range(cams):
            strip = (t + 1) % STRIPS + tile_step
            cam = c + cam_step
            if 0 <= strip < STRIPS and 0 <= cam < cams:
                pairs.append((t * cams + c, (t + tile_step) % tiles * cams + cam))
    return lax.ppermute(block, ("tile", "cam"), pairs)


def per_device(
    pixels,
    pixel_hidden,
    pixel_upstream,
    points,
    point_hidden,
    point_upstream,
    mixing,
    neighbors,
    send_list,
    pixel_weight,
    point_weight,
    kernel,
):
    tiles = lax.axis_size("tile")
    cams = lax.axis_size("cam")
    devices = tiles * cams
    slots = devices * CAP
    peers = [[peer_at(p) for p in range(devices)]]
    targets = jnp.transpose(send_list, (0, 2, 1))
    reads = neighbors.T
    blocks = (BLK_DEV, BS, C)
    outgoing, point_slope = pack(
        targets,
        points.reshape(blocks),
        point_hidden.reshape(blocks),
        point_upstream.reshape(blocks),
        devices,
    )
    outgoing, reads = lax.optimization_barrier((outgoing, reads))
    incoming = lax.all_to_all(
        outgoing,
        ("tile", "cam"),
        split_axis=0,
        concat_axis=0,
        tiled=True,
        axis_index_groups=peers,
    )
    pixel_slope, mixed, sums, first, last = pixel_part(
        reads, pixel_hidden, pixel_upstream, mixing, pixel_weight, slots
    )
    move = functools.partial(shifted, tiles=tiles, cams=cams)
    above = move(pixel_slope[-1:], tile_step=0, cam_step=1)
    below = move(pixel_slope[:1], tile_step=0, cam_step=-1)
    rim_left = move(last, tile_step=1, cam_step=0)
    rim_right = move(first, tile_step=-1, cam_step=0)
    sums, incoming, above, below, rim_left, rim_right, point_slope = lax.optimization_barrier(
        (sums, incoming, above, below, rim_left, rim_right, point_slope)
    )
    received = lax.all_to_all(
        sums.reshape(devices, CAP, BS, C),
        ("tile", "cam"),
        split_axis=0,
        concat_axis=0,
        tiled=True,
        axis_index_groups=peers,
    )
    base = point_upstream.astype(jnp.float32) + jnp.dot(
        point_slope.reshape(BLK_DEV * BS, C), point_weight.T, preferred_element_type=jnp.float32
    )
    base, first, last = lax.optimization_barrier((base, first, last))
    corners = (
        move(last[-1:], tile_step=1, cam_step=1),
        move(first[-1:], tile_step=-1, cam_step=1),
        move(last[:1], tile_step=1, cam_step=-1),
        move(first[:1], tile_step=-1, cam_step=-1),
    )
    mixing_gradient, pixel_gradient, totals = main_part(
        reads, incoming, mixed, pixels, mixing, pixel_upstream,
        pixel_slope, above, below, rim_left, rim_right, kernel,
    )
    gains = jnp.stack([kernel[2, 2], kernel[2, 0], kernel[0, 2], kernel[0, 0]])
    point_gradient, pixel_gradient = return_part(
        targets, received, base.reshape(blocks), totals, gains, corners, pixel_gradient
    )
    return (pixel_gradient, point_gradient.reshape(BLK_DEV * BS, C), mixing_gradient)


def solution(mesh):
    return jax.shard_map(
        per_device,
        mesh=mesh,
        in_specs=(
            P("cam", "tile", None),
            P("cam", "tile", None),
            P("cam", "tile", None),
            P(("tile", "cam"), None),
            P(("tile", "cam"), None),
            P(("tile", "cam"), None),
            P(("tile", "cam"), None, None),
            P(("tile", "cam"), None),
            P(("tile", "cam"), None, None),
            P(),
            P(),
            P(),
        ),
        out_specs=(
            P("cam", "tile", None),
            P(("tile", "cam"), None),
            P(("tile", "cam"), None, None),
        ),
        check_vma=False,
    )
```

```python
import functools

import jax
import jax.numpy as jnp
from jax import lax
from jax.experimental import pallas as pl
from jax.experimental.pallas import tpu as pltpu
from jax.sharding import PartitionSpec as P

C = 128
ROWS_DEV = 64
COLS_DEV = 128
K = 6
BS = 64
CAP = 2
BLK_DEV = 32
PB = 32
PIXB = 256
STRIPS = 4
MIB = 1024 * 1024
VMEM = 60 * MIB
DESTS = 4
OWNERS = 16
SPREAD = 2


def peer_at(position):
    return (position & 7) | ((position & 24) << 2) | ((position >> 2) & 24)


position_of = peer_at


def slope_of(upstream, hidden):
    argument = hidden.astype(jnp.float32)
    logistic = 0.5 + 0.5 * jnp.tanh(0.5 * argument)
    slope = logistic * (1.0 + argument * (1.0 - logistic))
    return (upstream.astype(jnp.float32) * slope).astype(jnp.bfloat16)


def pack_kernel(targets, points, hidden, upstream, out, slope, sem):
    def send(source, first):
        def body(i, carry):
            for j in range(DESTS):
                d = i * DESTS + j
                for s in range(CAP):
                    block = source.at[targets[0, s, peer_at(d)]]
                    pltpu.make_async_copy(block, out.at[d, first + s], sem).start()
            return carry

        lax.fori_loop(0, out.shape[0] // DESTS, body, 0)

    def fill(i, carry):
        part = pl.ds(2 * i, 2)
        slope[part] = slope_of(upstream[part], hidden[part])
        return carry

    send(points, 0)
    lax.fori_loop(0, BLK_DEV // 2, fill, 0)
    send(slope, CAP)
    pltpu.make_async_copy(out, out, sem).wait()


def pack(targets, points, hidden, upstream, devices):
    whole = pl.BlockSpec(memory_space=pltpu.VMEM)
    return pl.pallas_call(
        pack_kernel,
        in_specs=[pl.BlockSpec(memory_space=pltpu.SMEM), whole, whole, whole],
        out_specs=[pl.BlockSpec(memory_space=pl.ANY), whole],
        out_shape=[
            jax.ShapeDtypeStruct((devices, 2 * CAP, BS, C), jnp.bfloat16),
            jax.ShapeDtypeStruct((BLK_DEV, BS, C), jnp.bfloat16),
        ],
        scratch_shapes=[pltpu.SemaphoreType.DMA(())],
        compiler_params=pltpu.CompilerParams(vmem_limit_bytes=VMEM),
        cost_estimate=pl.CostEstimate(flops=10 * MIB, bytes_accessed=12 * MIB, transcendentals=0),
        name="pack",
    )(targets, points, hidden, upstream)


def pixel_kernel(
    neighbors, hidden, upstream, mixing, weight, slope, mixed, sums, first, last, total
):
    q = pl.program_id(0)

    @pl.when(q == 0)
    def _():
        total[...] = jnp.zeros_like(total)

    values = slope_of(upstream[...], hidden[...])
    slope[...] = values
    wide = values.astype(jnp.float32)
    for r in range(2):
        first[pl.ds(2 * q + r, 1), :] = wide[r, 0:1, :]
        last[pl.ds(2 * q + r, 1), :] = wide[r, COLS_DEV - 1 : COLS_DEV, :]
    projected = lax.dot_general(
        values.reshape(PIXB, C),
        weight[...],
        (((1,), (1,)), ((), ())),
        preferred_element_type=jnp.float32,
    ).astype(jnp.bfloat16)
    mixed[0] = projected
    term = lax.dot_general(
        mixing[0], projected, (((0,), (0,)), ((), ())), preferred_element_type=jnp.float32
    )
    for k in range(K):
        slot = position_of(lax.div(neighbors[k, q], CAP)) * CAP + lax.rem(neighbors[k, q], CAP)
        total[slot] += term[k * BS : (k + 1) * BS]

    @pl.when(q == PB - 1)
    def _():
        def body(i, carry):
            sums[i] = total[i].astype(jnp.bfloat16)
            return carry

        lax.fori_loop(0, total.shape[0], body, 0)


def pixel_part(neighbors, hidden, upstream, mixing, weight, slots):
    rows = pl.BlockSpec((2, COLS_DEV, C), lambda q, n: (q, 0, 0))
    return pl.pallas_call(
        pixel_kernel,
        grid_spec=pltpu.PrefetchScalarGridSpec(
            num_scalar_prefetch=1,
            grid=(PB,),
            in_specs=[
                rows,
                rows,
                pl.BlockSpec((1, PIXB, K * BS), lambda q, n: (q, 0, 0)),
                pl.BlockSpec((C, C), lambda q, n: (0, 0)),
            ],
            out_specs=[
                rows,
                pl.BlockSpec((1, PIXB, C), lambda q, n: (q, 0, 0)),
                pl.BlockSpec((slots, BS, C), lambda q, n: (0, 0, 0)),
                pl.BlockSpec((ROWS_DEV, C), lambda q, n: (0, 0)),
                pl.BlockSpec((ROWS_DEV, C), lambda q, n: (0, 0)),
            ],
            scratch_shapes=[pltpu.VMEM((slots, BS, C), jnp.float32)],
        ),
        out_shape=[
            jax.ShapeDtypeStruct((ROWS_DEV, COLS_DEV, C), jnp.bfloat16),
            jax.ShapeDtypeStruct((PB, PIXB, C), jnp.bfloat16),
            jax.ShapeDtypeStruct((slots, BS, C), jnp.bfloat16),
            jax.ShapeDtypeStruct((ROWS_DEV, C), jnp.float32),
            jax.ShapeDtypeStruct((ROWS_DEV, C), jnp.float32),
        ],
        compiler_params=pltpu.CompilerParams(vmem_limit_bytes=VMEM),
        cost_estimate=pl.CostEstimate(
            flops=1200 * MIB, bytes_accessed=18 * MIB, transcendentals=MIB
        ),
        name="pixel_part",
    )(neighbors, hidden, upstream, mixing, weight)


def main_kernel(
    neighbors, incoming, mixed, pixels, mixing, upstream, slope, above, below, left, right, kernel,
    mixing_gradient, pixel_gradient, totals, left_side, right_side,
):
    q = pl.program_id(0)
    for k in range(K):
        slot = neighbors[k, q]
        owner = position_of(lax.div(slot, CAP))
        place = lax.rem(slot, CAP)
        right_side[k * BS : (k + 1) * BS, 0:C] = incoming[owner, place]
        right_side[k * BS : (k + 1) * BS, C : 2 * C] = incoming[owner, CAP + place]
    left_side[:, 0:C] = mixed[0]
    left_side[:, C : 2 * C] = pixels[...].reshape(PIXB, C)
    mixing_gradient[0] = lax.dot_general(
        left_side[...],
        right_side[...],
        (((1,), (1,)), ((), ())),
        preferred_element_type=jnp.float32,
    ).astype(jnp.bfloat16)
    term = jnp.dot(mixing[0], right_side[:, C : 2 * C], preferred_element_type=jnp.float32)
    column = lax.broadcasted_iota(jnp.int32, (COLS_DEV, C), 0)
    before = jnp.maximum(2 * q - 1, 0)
    after = jnp.minimum(2 * q + 2, ROWS_DEV - 1)
    top = q == 0
    bottom = q == PB - 1

    def wide(piece):
        return piece.astype(jnp.float32)

    rows = [
        jnp.where(top, wide(above[0]), wide(slope[before])),
        wide(slope[2 * q]),
        wide(slope[2 * q + 1]),
        jnp.where(bottom, wide(below[0]), wide(slope[after])),
    ]

    def rim(side):
        zero = jnp.zeros((1, C), jnp.float32)
        return [
            jnp.where(top, zero, side[pl.ds(before, 1), :]),
            side[pl.ds(2 * q, 1), :],
            side[pl.ds(2 * q + 1, 1), :],
            jnp.where(bottom, zero, side[pl.ds(after, 1), :]),
        ]

    rims = {0: rim(right), 2: rim(left)}
    gains = [[kernel[a, e : e + 1, :] for e in range(3)] for a in range(3)]

    def mix(pieces, r, e):
        return sum(gains[a][e] * pieces[r + 2 - a] for a in range(3))

    for r in range(2):
        total = wide(upstream[r]) + term[r * COLS_DEV : (r + 1) * COLS_DEV]
        total = total + mix(rows, r, 1)
        ahead = pltpu.roll(mix(rows, r, 0), COLS_DEV - 1, 0)
        total = total + jnp.where(column == COLS_DEV - 1, mix(rims[0], r, 0), ahead)
        behind = pltpu.roll(mix(rows, r, 2), 1, 0)
        total = total + jnp.where(column == 0, mix(rims[2], r, 2), behind)
        pixel_gradient[r] = total.astype(jnp.bfloat16)

        @pl.when(q == r * (PB - 1))
        def _():
            totals[2 * r : 2 * r + 1] = total[0:1]
            totals[2 * r + 1 : 2 * r + 2] = total[COLS_DEV - 1 : COLS_DEV]


def main_part(
    neighbors, incoming, mixed, pixels, mixing, upstream, slope, above, below, left, right, kernel
):
    rows = pl.BlockSpec((2, COLS_DEV, C), lambda q, n: (q, 0, 0))
    once = pl.Buffered(1)
    return pl.pallas_call(
        main_kernel,
        grid_spec=pltpu.PrefetchScalarGridSpec(
            num_scalar_prefetch=1,
            grid=(PB,),
            in_specs=[
                pl.BlockSpec(incoming.shape, lambda q, n: (0, 0, 0, 0), pipeline_mode=once),
                pl.BlockSpec((1, PIXB, C), lambda q, n: (q, 0, 0)),
                rows,
                pl.BlockSpec((1, PIXB, K * BS), lambda q, n: (q, 0, 0)),
                rows,
                pl.BlockSpec(slope.shape, lambda q, n: (0, 0, 0), pipeline_mode=once),
                pl.BlockSpec(above.shape, lambda q, n: (0, 0, 0)),
                pl.BlockSpec(below.shape, lambda q, n: (0, 0, 0)),
                pl.BlockSpec(left.shape, lambda q, n: (0, 0)),
                pl.BlockSpec(right.shape, lambda q, n: (0, 0)),
                pl.BlockSpec((3, 3, C), lambda q, n: (0, 0, 0)),
            ],
            out_specs=[
                pl.BlockSpec((1, PIXB, K * BS), lambda q, n: (q, 0, 0)),
                rows,
                pl.BlockSpec((4, C), lambda q, n: (0, 0)),
            ],
            scratch_shapes=[
                pltpu.VMEM((PIXB, 2 * C), jnp.bfloat16),
                pltpu.VMEM((K * BS, 2 * C), jnp.bfloat16),
            ],
        ),
        out_shape=[
            jax.ShapeDtypeStruct((PB, PIXB, K * BS), jnp.bfloat16),
            jax.ShapeDtypeStruct((ROWS_DEV, COLS_DEV, C), jnp.bfloat16),
            jax.ShapeDtypeStruct((4, C), jnp.float32),
        ],
        compiler_params=pltpu.CompilerParams(vmem_limit_bytes=VMEM),
        cost_estimate=pl.CostEstimate(
            flops=2600 * MIB, bytes_accessed=30 * MIB, transcendentals=0
        ),
        name="main_part",
    )(
        neighbors, incoming, mixed, pixels, mixing, upstream, slope, above, below, left, right,
        kernel,
    )


def return_kernel(
    targets, received, base, totals, gains, corner_0, corner_1, corner_2, corner_3, gradient,
    out, fixed, landed, sems, tiles, tile_sems, start, start_sem, *sums,
):
    parts = received.shape[0] // OWNERS

    def fetch(i):
        part = pl.ds(i * OWNERS, OWNERS)
        return pltpu.make_async_copy(received.at[part], landed.at[part], sems.at[i])

    def place(ref, i):
        return ref.at[i // 2 * (ROWS_DEV - 1), pl.ds(i % 2 * (COLS_DEV - 16), 16)]

    def load(i):
        return pltpu.make_async_copy(place(gradient, i), tiles.at[i], tile_sems.at[i])

    def store(i):
        return pltpu.make_async_copy(tiles.at[i], place(fixed, i), tile_sems.at[i])

    for i in range(4):
        load(i).start()
    for i in range(parts):
        fetch(i).start()
    first = pltpu.make_async_copy(base, start, start_sem)
    first.start()
    for total in sums:
        total[...] = jnp.zeros_like(total)
    row = lax.broadcasted_iota(jnp.int32, (16, C), 0)
    for i, corner in enumerate((corner_0, corner_1, corner_2, corner_3)):
        load(i).wait()
        value = totals[i : i + 1, :] + gains[i : i + 1, :] * corner[...]
        tile = jnp.where(row == i % 2 * 15, value, tiles[i].astype(jnp.float32))
        tiles[i] = tile.astype(jnp.bfloat16)
        store(i).start()

    def body(i, carry):
        fetch(i).wait()
        for j in range(OWNERS):
            for s in range(CAP):
                o = i * OWNERS + j
                block = targets[0, s, peer_at(o)]
                sums[(j * CAP + s) % SPREAD][block] += landed[o, s].astype(jnp.float32)
        return carry

    lax.fori_loop(0, parts, body, 0)
    first.wait()
    whole = start[...]
    for total in sums:
        whole = whole + total[...]
    out[...] = whole.astype(jnp.bfloat16)
    for i in range(4):
        store(i).wait()


def return_part(targets, received, base, totals, gains, corners, gradient):
    whole = pl.BlockSpec(memory_space=pltpu.VMEM)
    anywhere = pl.BlockSpec(memory_space=pl.ANY)
    parts = received.shape[0] // OWNERS
    return pl.pallas_call(
        return_kernel,
        in_specs=[pl.BlockSpec(memory_space=pltpu.SMEM), anywhere, anywhere]
        + [whole] * 6
        + [anywhere],
        out_specs=[whole, anywhere],
        scratch_shapes=[
            pltpu.VMEM(received.shape, jnp.bfloat16),
            pltpu.SemaphoreType.DMA((parts,)),
            pltpu.VMEM((4, 16, C), jnp.bfloat16),
            pltpu.SemaphoreType.DMA((4,)),
            pltpu.VMEM((BLK_DEV, BS, C), jnp.float32),
            pltpu.SemaphoreType.DMA(()),
        ]
        + [pltpu.VMEM((BLK_DEV, BS, C), jnp.float32)] * SPREAD,
        out_shape=[
            jax.ShapeDtypeStruct((BLK_DEV, BS, C), jnp.bfloat16),
            jax.ShapeDtypeStruct(gradient.shape, jnp.bfloat16),
        ],
        input_output_aliases={9: 1},
        compiler_params=pltpu.CompilerParams(vmem_limit_bytes=VMEM),
        cost_estimate=pl.CostEstimate(flops=4 * MIB, bytes_accessed=6 * MIB, transcendentals=0),
        name="return_part",
    )(targets, received, base, totals, gains, *corners, gradient)


def shifted(block, tiles, cams, tile_step, cam_step):
    pairs = []
    for t in range(tiles):
        for c in range(cams):
            strip = (t + 1) % STRIPS + tile_step
            cam = c + cam_step
            if 0 <= strip < STRIPS and 0 <= cam < cams:
                pairs.append((t * cams + c, (t + tile_step) % tiles * cams + cam))
    return lax.ppermute(block, ("tile", "cam"), pairs)


def per_device(
    pixels,
    pixel_hidden,
    pixel_upstream,
    points,
    point_hidden,
    point_upstream,
    mixing,
    neighbors,
    send_list,
    pixel_weight,
    point_weight,
    kernel,
):
    tiles = lax.axis_size("tile")
    cams = lax.axis_size("cam")
    devices = tiles * cams
    slots = devices * CAP
    peers = [[peer_at(p) for p in range(devices)]]
    targets = jnp.transpose(send_list, (0, 2, 1))
    reads = neighbors.T
    blocks = (BLK_DEV, BS, C)
    outgoing, point_slope = pack(
        targets,
        points.reshape(blocks),
        point_hidden.reshape(blocks),
        point_upstream.reshape(blocks),
        devices,
    )
    outgoing, reads = lax.optimization_barrier((outgoing, reads))
    incoming = lax.all_to_all(
        outgoing,
        ("tile", "cam"),
        split_axis=0,
        concat_axis=0,
        tiled=True,
        axis_index_groups=peers,
    )
    pixel_slope, mixed, sums, first, last = pixel_part(
        reads, pixel_hidden, pixel_upstream, mixing, pixel_weight, slots
    )
    move = functools.partial(shifted, tiles=tiles, cams=cams)
    above = move(pixel_slope[-1:], tile_step=0, cam_step=1)
    below = move(pixel_slope[:1], tile_step=0, cam_step=-1)
    rim_left = move(last, tile_step=1, cam_step=0)
    rim_right = move(first, tile_step=-1, cam_step=0)
    sums, incoming, above, below, rim_left, rim_right, point_slope = lax.optimization_barrier(
        (sums, incoming, above, below, rim_left, rim_right, point_slope)
    )
    received = lax.all_to_all(
        sums.reshape(devices, CAP, BS, C),
        ("tile", "cam"),
        split_axis=0,
        concat_axis=0,
        tiled=True,
        axis_index_groups=peers,
    )
    base = point_upstream.astype(jnp.float32) + jnp.dot(
        point_slope.reshape(BLK_DEV * BS, C), point_weight.T, preferred_element_type=jnp.float32
    )
    base, first, last = lax.optimization_barrier((base, first, last))
    corners = (
        move(last[-1:], tile_step=1, cam_step=1),
        move(first[-1:], tile_step=-1, cam_step=1),
        move(last[:1], tile_step=1, cam_step=-1),
        move(first[:1], tile_step=-1, cam_step=-1),
    )
    mixing_gradient, pixel_gradient, totals = main_part(
        reads, incoming, mixed, pixels, mixing, pixel_upstream,
        pixel_slope, above, below, rim_left, rim_right, kernel,
    )
    gains = jnp.stack([kernel[2, 2], kernel[2, 0], kernel[0, 2], kernel[0, 0]])
    point_gradient, pixel_gradient = return_part(
        targets, received, base.reshape(blocks), totals, gains, corners, pixel_gradient
    )
    return (pixel_gradient, point_gradient.reshape(BLK_DEV * BS, C), mixing_gradient)


def solution(mesh):
    return jax.shard_map(
        per_device,
        mesh=mesh,
        in_specs=(
            P("cam", "tile", None),
            P("cam", "tile", None),
            P("cam", "tile", None),
            P(("tile", "cam"), None),
            P(("tile", "cam"), None),
            P(("tile", "cam"), None),
            P(("tile", "cam"), None, None),
            P(("tile", "cam"), None),
            P(("tile", "cam"), None, None),
            P(),
            P(),
            P(),
        ),
        out_specs=(
            P("cam", "tile", None),
            P(("tile", "cam"), None),
            P(("tile", "cam"), None, None),
        ),
        check_vma=False,
    )
```
